32 devices in a mesh: req: 8 (over z, y), fsdp: 4 (over x, core).
Axes of the slice: x: 2, y: 2, z: 4, core: 2. Of those that a mesh axis runs over, the one named last changes fastest.
Arguments:
- stretch_x: bfloat16 [16, 2048, 1024], P('req', 'fsdp'), may hold values from -6 to 6
- dec_x: bfloat16 [32, 1024], P('req'), may hold values from -6 to 6
- w_qkv: bfloat16 [1024, 3072], P(('req', 'fsdp')), may hold values from -1 to 1, as said below
- w_out: bfloat16 [1024, 1024], P(('req', 'fsdp')), may hold values from -0.375 to 0.375
- w_loc: bfloat16 [1024, 128], P(('req', 'fsdp')), may hold values from -0.1875 to 0.1875
- w_mix: bfloat16 [1024, 4], P(('req', 'fsdp')), may hold values from -30 to 30
- attn_gain: float32 [1024], replicated, may hold values from 0.1 to 1.9
- bias_same: float32 [16], replicated, may hold values from -3 to 3
- bias_diff: float32 [16], replicated, may hold values from -3 to 3
- cache_kv: bfloat16 [32, 4096, 2048], P('req', 'fsdp'), may hold values from -40 to 40, as said below
- prompt_kv: bfloat16 [4, 1024, 2048], P(None, 'fsdp'), may hold values from -40 to 40, as said below
- stretch_len: int32 [16], P('req'), may hold values from 1 to 2048, 24576 in all
- cache_len: int32 [32], P('req'), may hold values from 1 to 4096, 81920 in all
- prompt_group: int32 [32], P('req'), may hold values from 0 to 3
- pre_variate: int32 [16, 2048], P('req'), may hold values from 0 to 3
- dec_variate: int32 [32], P('req'), may hold values from 0 to 3
- cache_variate: int32 [32, 4096], P('req', 'fsdp'), may hold values from 0 to 3
- prompt_variate: int32 [4, 1024], P(None, 'fsdp'), may hold values from 0 to 3
Outputs:
- pre_out: bfloat16 [16, 2048, 1024], P('req', 'fsdp')
- dec_out: bfloat16 [32, 1024], P('req')
- pre_fore: float32 [16, 2048, 32], P('req', 'fsdp')
- dec_fore: float32 [32, 32], P('req')
The draws below stay inside these ranges and needn't reach their ends.
Inputs may be any that keep to these rules, and one draw needn't show every extreme that they name: `stretch_len`: the longest stretch has exactly 2048 valid patches. `cache_len`: the longest cache has exactly 4096 valid patches. `w_qkv`: independent entries. `cache_kv`: independent entries. `prompt_kv`: independent entries.
All inputs are finite; a program needn't handle non-finite values. No bound on the sum of `stretch_len` or of `cache_len` on one device may be relied on, other than what follows from the above.
Results may differ from the reference program's by a relative error of at most 0.012.
The reference program's roundings to bfloat16 on the way (of `normed`, `projected`, `pre_attn`, `dec_attn` and `scaled`) count: a program that leaves them out, or rounds other values in their place, can miss the bound.
Values may be sent and summed in bfloat16 or wider, within the bound.
No kernel may reach another device: no remote copies, remote signals or barrier semaphores. Data moves between devices by JAX's collectives and lax.ppermute only.
A program may use at most 128 MiB of HBM per device.

```python
import math
import jax
import jax.numpy as jnp
import numpy as np
from jax import lax

EMBED_WIDTH = 1024
H = 16
HD = 64
BLEND_TERMS = 4
STEPS_PER_PIECE = 32
NVAR = 4
PIECES_PER_PROMPT = 2048
CACHE = 4096
PROMPT = 1024
PGROUPS = 4
PROMPT_RUNS = 16
DECODES = 32


def draw_w_qkv(key, part):
    entries = jax.random.truncated_normal(key, -4.0, 4.0, (EMBED_WIDTH, 3 * EMBED_WIDTH), jnp.float32) / math.sqrt(EMBED_WIDTH)
    return entries.astype(jnp.bfloat16)


def draw_w_mix(key, part):
    own_key = jax.random.fold_in(jax.random.fold_in(key, 5), 1)
    entries = jax.random.truncated_normal(own_key, -4.0, 4.0, (EMBED_WIDTH, BLEND_TERMS), jnp.float32) / math.sqrt(EMBED_WIDTH)
    return entries.astype(jnp.bfloat16)


def draw_pairs(key, leading):
    first_key, second_key = jax.random.split(key)
    key_part = jax.random.truncated_normal(first_key, -4.0, 4.0, leading + (EMBED_WIDTH,), jnp.float32)
    value_part = jax.random.truncated_normal(second_key, -4.0, 4.0, leading + (EMBED_WIDTH,), jnp.float32)
    return jnp.concatenate([key_part, value_part], axis=-1).astype(jnp.bfloat16)


def draw_cache_kv(key, part):
    return draw_pairs(jax.random.fold_in(key, 11), (DECODES, CACHE))


def draw_prompt_kv(key, part):
    return draw_pairs(jax.random.fold_in(key, 23), (PGROUPS, PROMPT))


def set_ends(drawn, rng, low, largest):
    longest = drawn.shape.index(max(drawn.shape))
    spots = []
    for shift in (0, 1):
        where = [jax.random.randint(jax.random.fold_in(rng, axis), (), 0, length) for axis, length in enumerate(drawn.shape)]
        where[longest] = (where[longest] + shift) % drawn.shape[longest]
        spots.append(tuple(where))
    return drawn.at[spots[0]].set(low).at[spots[1]].set(largest)


def level_of(stream_key, dims, cuts, low, largest):
    def one(axis_at, blocks):
        draws = jax.random.uniform(jax.random.fold_in(jax.random.fold_in(stream_key, 6), axis_at), (blocks,), jnp.float32, low / len(cuts), largest / len(cuts))
        return jnp.repeat(jnp.exp(draws), dims[axis_at] // blocks).reshape((-1,) + (1,) * (len(dims) - axis_at - 1))

    loudness = one(*cuts[0])
    for cut in cuts[1:]:
        loudness = loudness * one(*cut)
    return loudness


def profile(amount, total, bound, skew):
    weights = [(1 << 20) // math.isqrt(rank ** skew) + 1 for rank in range(2, amount + 1)]
    rest, holding = total - bound - (amount - 1), [1] * (amount - 1)
    while rest > 0:
        candidates = [i for i in range(amount - 1) if holding[i] < bound]
        whole, budget = sum([weights[i] for i in candidates]), rest
        for i in candidates:
            addition = min(bound - holding[i], max(1, budget * weights[i] // whole), rest)
            holding[i] = holding[i] + addition
            rest = rest - addition
    return np.array([bound] + holding)


def ragged(rng, number_of, total, limit, lean):
    if number_of == 2:
        one = jax.random.randint(rng, (), max(1, total - limit), min(limit, total - 1) + 1)
        return jnp.stack([one, total - one])
    lengths = jnp.asarray(profile(number_of, total, limit, lean), jnp.int32)
    twos = (number_of - 1) // 2
    source_of, sink = lengths[1:1 + 2 * twos:2], lengths[2:2 + 2 * twos:2]
    room = jnp.minimum(source_of - 1, limit - sink)
    shifted = jax.random.randint(jax.random.fold_in(rng, 1), (twos,), 0, 1 << 20) % (room + 1)
    lengths = lengths.at[1:1 + 2 * twos:2].set(source_of - shifted).at[2:2 + 2 * twos:2].set(sink + shifted)
    return lengths[jax.random.permutation(jax.random.fold_in(rng, 2), number_of)]


def bell_draw(key, extent, scale, limit, pieces=(), held_as=jnp.bfloat16):
    drawn = scale * jax.random.normal(key, extent, jnp.float32)
    if pieces:
        drawn = drawn * level_of(key, extent, pieces, -0.22, 0.18)
    return jnp.clip(drawn, -limit, limit).astype(held_as)


def setup_inputs(seed: int = 0) -> dict:
    key_of = jax.random.split(jax.random.key(seed), 19)
    stretch_x = bell_draw(key_of[0], (PROMPT_RUNS, PIECES_PER_PROMPT, EMBED_WIDTH), 1.0, 6.0, ((0, 8), (1, 4)))
    dec_x = bell_draw(key_of[1], (DECODES, EMBED_WIDTH), 1.0, 6.0, ((0, 8),))
    w_qkv = draw_w_qkv(jax.random.fold_in(key_of[18], 71), 0)
    w_out = bell_draw(key_of[3], (EMBED_WIDTH, EMBED_WIDTH), (EMBED_WIDTH // 4) ** -0.5, 0.375, ((0, 32),))
    w_loc = bell_draw(key_of[4], (EMBED_WIDTH, BLEND_TERMS * STEPS_PER_PIECE), EMBED_WIDTH ** -0.5, 0.1875, ((0, 32),))
    w_mix = draw_w_mix(jax.random.fold_in(key_of[18], 71), 0)
    attn_gain = jnp.clip(1.0 + 0.18 * jax.random.normal(key_of[6], (EMBED_WIDTH,), jnp.float32), 0.1, 1.9)
    bias_same = jnp.clip(jax.random.uniform(key_of[7], (H,), jnp.float32, -3.0, 3.0), -3.0, 3.0)
    bias_diff = jnp.clip(jax.random.uniform(key_of[8], (H,), jnp.float32, -3.0, 3.0), -3.0, 3.0)
    cache_kv = draw_cache_kv(jax.random.fold_in(key_of[18], 71), 0)
    prompt_kv = draw_prompt_kv(jax.random.fold_in(key_of[18], 71), 0)
    stretch_len = ragged(key_of[11], PROMPT_RUNS, PROMPT_RUNS * PIECES_PER_PROMPT * 3 // 4, PIECES_PER_PROMPT, 1).astype(jnp.int32)
    cache_len = ragged(key_of[12], DECODES, DECODES * CACHE * 5 // 8, CACHE, 1).astype(jnp.int32)
    prompt_group = set_ends(jax.random.randint(key_of[13], (DECODES,), 0, PGROUPS), jax.random.fold_in(key_of[13], 1), 0, PGROUPS - 1).astype(jnp.int32)
    pre_variate = set_ends(jax.random.randint(key_of[14], (PROMPT_RUNS, PIECES_PER_PROMPT), 0, NVAR), jax.random.fold_in(key_of[14], 1), 0, NVAR - 1).astype(jnp.int32)
    dec_variate = set_ends(jax.random.randint(key_of[15], (DECODES,), 0, NVAR), jax.random.fold_in(key_of[15], 1), 0, NVAR - 1).astype(jnp.int32)
    cache_variate = set_ends(jax.random.randint(key_of[16], (DECODES, CACHE), 0, NVAR), jax.random.fold_in(key_of[16], 1), 0, NVAR - 1).astype(jnp.int32)
    prompt_variate = set_ends(jax.random.randint(key_of[17], (PGROUPS, PROMPT), 0, NVAR), jax.random.fold_in(key_of[17], 1), 0, NVAR - 1).astype(jnp.int32)
    return dict(stretch_x=stretch_x, dec_x=dec_x, w_qkv=w_qkv, w_out=w_out, w_loc=w_loc, w_mix=w_mix, attn_gain=attn_gain, bias_same=bias_same, bias_diff=bias_diff, cache_kv=cache_kv, prompt_kv=prompt_kv, stretch_len=stretch_len, cache_len=cache_len, prompt_group=prompt_group, pre_variate=pre_variate, dec_variate=dec_variate, cache_variate=cache_variate, prompt_variate=prompt_variate)


epsilon = 1e-05
big_negative = -1e+30

def rms_scale(rows, gain):
    as_float = rows.astype(jnp.float32)
    factor = lax.rsqrt(lax.optimization_barrier(jnp.mean(as_float * as_float, axis=-1, keepdims=True)) + epsilon)
    return (as_float * factor * gain).astype(jnp.bfloat16)

def softmax_mix(scores, valid_mask, value_rows):
    masked = jnp.where(valid_mask, scores, big_negative)
    row_max = lax.optimization_barrier(jnp.max(masked, axis=-1, keepdims=True))
    weights = jnp.where(valid_mask, jnp.exp(scores - row_max), 0.0)
    row_sum = lax.optimization_barrier(jnp.sum(weights, axis=-1))
    rounded = lax.optimization_barrier(weights.astype(jnp.bfloat16)).astype(jnp.float32)
    mixed = jnp.einsum('hqk,khe->qhe', rounded, value_rows.astype(jnp.float32))
    return mixed / jnp.transpose(row_sum)[:, :, None]

def reference(stretch_x, dec_x, w_qkv, w_out, w_loc, w_mix, attn_gain, bias_same, bias_diff, cache_kv, prompt_kv, stretch_len, cache_len, prompt_group, pre_variate, dec_variate, cache_variate, prompt_variate):
    scaling = 1.0 / math.sqrt(HD)
    prompt_token_sum = PROMPT_RUNS * PIECES_PER_PROMPT
    inputs = jnp.concatenate([stretch_x.reshape(prompt_token_sum, EMBED_WIDTH), dec_x], axis=0)
    normed = rms_scale(inputs, attn_gain)
    projected = jnp.dot(normed, w_qkv, preferred_element_type=jnp.float32).astype(jnp.bfloat16)
    queries = projected[:, :EMBED_WIDTH].reshape(-1, H, HD)
    key_rows = projected[:, EMBED_WIDTH:2 * EMBED_WIDTH].reshape(-1, H, HD)
    value_rows = projected[:, 2 * EMBED_WIDTH:].reshape(-1, H, HD)
    positions = jnp.arange(PIECES_PER_PROMPT, dtype=jnp.int32)

    def one_stretch(packed):
        stretch_q, stretch_k, stretch_v, stretch_length, variates = packed
        scores = jnp.einsum('qhe,khe->hqk', stretch_q.astype(jnp.float32), stretch_k.astype(jnp.float32)) * scaling
        same_mask = variates[:, None] == variates[None, :]
        scores = scores + jnp.where(same_mask[None], bias_same[:, None, None], bias_diff[:, None, None])
        valid_mask = (positions[None, :] <= positions[:, None]) & (positions[None, :] < stretch_length)
        return softmax_mix(scores, valid_mask[None], stretch_v).astype(jnp.bfloat16)
    pre_attn = lax.map(one_stretch, (queries[:prompt_token_sum].reshape(PROMPT_RUNS, PIECES_PER_PROMPT, H, HD), key_rows[:prompt_token_sum].reshape(PROMPT_RUNS, PIECES_PER_PROMPT, H, HD), value_rows[:prompt_token_sum].reshape(PROMPT_RUNS, PIECES_PER_PROMPT, H, HD), stretch_len, pre_variate))
    cache_positions = jnp.arange(CACHE, dtype=jnp.int32)

    def one_request(packed):
        req_q, req_k, req_v, req_length, group, variate, cache_rows, cache_vars = packed
        prompt_rows = prompt_kv[group]
        all_keys = jnp.concatenate([prompt_rows[:, :EMBED_WIDTH], cache_rows[:, :EMBED_WIDTH], req_k.reshape(1, EMBED_WIDTH)], axis=0).reshape(-1, H, HD)
        all_values = jnp.concatenate([prompt_rows[:, EMBED_WIDTH:], cache_rows[:, EMBED_WIDTH:], req_v.reshape(1, EMBED_WIDTH)], axis=0).reshape(-1, H, HD)
        key_vars = jnp.concatenate([prompt_variate[group], cache_vars, variate.reshape(1)], axis=0)
        valid_mask = jnp.concatenate([jnp.ones((PROMPT,), bool), cache_positions < req_length, jnp.ones((1,), bool)], axis=0)
        scores = jnp.einsum('he,nhe->hn', req_q.astype(jnp.float32), all_keys.astype(jnp.float32)) * scaling
        scores = scores + jnp.where((key_vars == variate)[None], bias_same[:, None], bias_diff[:, None])
        mixed = softmax_mix(scores[:, None, :], valid_mask[None, None, :], all_values)
        return mixed.reshape(EMBED_WIDTH).astype(jnp.bfloat16)
    dec_attn = lax.map(one_request, (queries[prompt_token_sum:], key_rows[prompt_token_sum:], value_rows[prompt_token_sum:], cache_len, prompt_group, dec_variate, cache_kv, cache_variate))
    attn_rows = jnp.concatenate([pre_attn.reshape(prompt_token_sum, EMBED_WIDTH), dec_attn], axis=0)
    block_results = (inputs.astype(jnp.float32) + jnp.dot(attn_rows, w_out, preferred_element_type=jnp.float32)).astype(jnp.bfloat16)
    scaled = rms_scale(block_results, 1.0)
    blend_centers = jnp.dot(scaled, w_loc, preferred_element_type=jnp.float32)
    blend_proportions = jax.nn.softmax(jnp.dot(scaled, w_mix, preferred_element_type=jnp.float32), axis=-1)
    prediction_readout = jnp.einsum('hj,hjg->hg', blend_proportions, blend_centers.reshape(-1, BLEND_TERMS, STEPS_PER_PIECE), precision=lax.Precision.HIGHEST)
    return (block_results[:prompt_token_sum].reshape(PROMPT_RUNS, PIECES_PER_PROMPT, EMBED_WIDTH), block_results[prompt_token_sum:], prediction_readout[:prompt_token_sum].reshape(PROMPT_RUNS, PIECES_PER_PROMPT, STEPS_PER_PIECE), prediction_readout[prompt_token_sum:])
```

```python
import functools
import math

import jax
import jax.numpy as jnp
from jax import lax
from jax.experimental import pallas as pl
from jax.experimental.pallas import tpu as pltpu
from jax.sharding import PartitionSpec as P

epsilon = 1e-05
big_negative = -1e30
log2e = math.log2(math.e)
F32 = jnp.float32
BF16 = jnp.bfloat16
ANY = pl.BlockSpec(memory_space=pl.ANY)
VMEM = pl.BlockSpec(memory_space=pltpu.VMEM)
NT = (((1,), (1,)), ((), ()))


def swap(value, axis, size, offset):
    return lax.ppermute(value, axis, [(i, i ^ offset) for i in range(size)])


def normalise(rows, gain):
    as_float = rows.astype(F32)
    factor = lax.rsqrt(jnp.mean(as_float * as_float, axis=-1, keepdims=True) + epsilon)
    scaled = as_float * factor
    return (scaled if gain is None else scaled * gain).astype(BF16)


def weight_copies(pieces, row_ref, sems, req_index, rows):
    copies = []
    for i, piece in enumerate(pieces):
        for j in range(piece.shape[0]):
            first = pl.multiple_of((req_index ^ (2 * j + i)) * rows, rows)
            copies.append(
                pltpu.make_async_copy(piece.at[j], row_ref.at[pl.ds(first, rows)], sems.at[len(copies)])
            )
    return copies


def attention_kernel(
    meta, *refs, pieces, chunks, weight_parts, own_slot, with_decode
):
    refs = list(refs)
    xs = [refs.pop(0) for _ in range(pieces)]
    weights = [[refs.pop(0) for _ in range(weight_parts)] for _ in range(chunks)]
    gain_ref, table_ref, variate_ref = refs.pop(0), refs.pop(0), refs.pop(0)
    dec_ref = refs.pop(0) if with_decode else None
    out_ref = refs.pop(0)
    dec_out_ref = refs.pop(0) if with_decode else None
    xbuf, wbuf, keys, values, key_extra, xsems, wsems = refs
    fsdp_index, req_index, length = meta[0], meta[1], meta[2]
    block = pl.program_id(0)
    rows = xbuf.shape[1]
    tile = math.gcd(rows, 256)

    def fetch(which, start):
        slot = which % 2
        if start:
            offset = which ^ fsdp_index
            for j in range(pieces):
                source = xs[j].at[own_slot] if j == 0 else xs[j]

                @pl.when(offset == j)
                def _():
                    pltpu.make_async_copy(source, xbuf.at[slot], xsems.at[slot]).start()
        else:
            pltpu.make_async_copy(xs[0].at[own_slot], xbuf.at[slot], xsems.at[slot]).wait()

    w_rows = wbuf.shape[1] // (weights[0][0].shape[0] * weight_parts)

    def w_copies():
        return [
            copy
            for c in range(chunks)
            for copy in weight_copies(weights[c], wbuf.at[c], wsems.at[c], req_index, w_rows)
        ]

    @pl.when(block == 0)
    def _():
        fetch(0, True)
        for copy in w_copies():
            copy.start()

    for c in range(pieces):

        @pl.when(block == c)
        def _(c=c):
            if c + 1 < pieces:
                fetch(c + 1, True)
            if c == 0:
                for copy in w_copies():
                    copy.wait()
                if with_decode:
                    dec_rows = normalise(dec_ref[...], gain_ref[...])
                    for n in range(chunks):
                        dec_out_ref[n] = jnp.dot(
                            dec_rows, wbuf[n], preferred_element_type=F32
                        ).astype(BF16)
            fetch(c, False)
            normed = normalise(xbuf[c % 2], gain_ref[...])
            here = pl.ds(c * rows, rows)
            lane = lax.broadcasted_iota(jnp.int32, (rows, 128), 1)
            low = lane < 64
            variate = jnp.broadcast_to(
                variate_ref[:, c * rows : (c + 1) * rows].astype(F32), (128, rows)
            ).T.astype(jnp.int32)
            same = (lane & 3) == variate
            position = c * rows + lax.broadcasted_iota(jnp.int32, (rows, 128), 0)
            extra = jnp.where(
                lane < 12,
                jnp.where(same, 1.0, 0.0),
                jnp.where((lane == 12) & (position >= length), big_negative, 0.0),
            )
            key_extra[here, :] = extra.astype(BF16)
            queries = []
            for n in range(chunks):
                projected = jnp.dot(normed, wbuf[n], preferred_element_type=F32).astype(BF16)
                q = projected[:, :128].astype(F32) * (log2e * 0.125)
                k = projected[:, 128:256].astype(F32)
                v = projected[:, 256:].astype(F32)
                q_high = q.astype(BF16).astype(F32)
                q_low = q - q_high
                q_high_turned = pltpu.roll(q_high, 64, 1)
                q_low_turned = pltpu.roll(q_low, 64, 1)
                k_turned = pltpu.roll(k, 64, 1)
                keys[2 * n, here, :] = jnp.where(low, k, k_turned).astype(BF16)
                keys[2 * n + 1, here, :] = jnp.where(low, k_turned, k).astype(BF16)
                values[2 * n, here, :] = jnp.where(low, v, 1.0).astype(BF16)
                values[2 * n + 1, here, :] = jnp.where(low, 1.0, v).astype(BF16)
                for half, q_main in (
                    (0, jnp.where(low, q_high, q_low_turned)),
                    (1, jnp.where(low, q_high_turned, q_low)),
                ):
                    bias = table_ref[2 * n + half]
                    q_extra = jnp.where(same, bias[0:1], bias[1:2])
                    queries.append(
                        jnp.concatenate([q_main.astype(BF16), q_extra.astype(BF16)], axis=1)
                    )
            diagonal = lax.broadcasted_iota(jnp.int32, (tile, tile), 1) <= lax.broadcasted_iota(
                jnp.int32, (tile, tile), 0
            )
            low_tile = lax.broadcasted_iota(jnp.int32, (tile, 128), 1) < 64
            for n in range(chunks):
                for t in range(rows // tile):
                    span = c * rows + (t + 1) * tile
                    mixed = []
                    for half in range(2):
                        head = 2 * n + half
                        query = queries[head][t * tile : (t + 1) * tile]
                        last = slice(span - tile, span)
                        s_last = lax.dot_general(
                            query,
                            jnp.concatenate([keys[head, last, :], key_extra[last, :]], axis=1),
                            NT,
                            preferred_element_type=F32,
                        )
                        s_last = jnp.where(diagonal, s_last, big_negative)
                        top = jnp.max(s_last, axis=1, keepdims=True)
                        if span > tile:
                            first = slice(0, span - tile)
                            s_first = lax.dot_general(
                                query,
                                jnp.concatenate([keys[head, first, :], key_extra[first, :]], axis=1),
                                NT,
                                preferred_element_type=F32,
                            )
                            top = jnp.maximum(top, jnp.max(s_first, axis=1, keepdims=True))
                        weights_last = jnp.exp2(s_last - top).astype(BF16)
                        total = jnp.dot(
                            weights_last, values[head, last, :], preferred_element_type=F32
                        )
                        if span > tile:
                            weights_first = jnp.exp2(s_first - top).astype(BF16)
                            total = total + jnp.dot(
                                weights_first, values[head, first, :], preferred_element_type=F32
                            )
                        mixed.append(total / pltpu.roll(total, 64, 1))
                    out_ref[t * tile : (t + 1) * tile, n * 128 : (n + 1) * 128] = jnp.where(
                        low_tile, mixed[0], mixed[1]
                    ).astype(BF16)


def attention(meta, xs, own_slot, weights, gain, table, variates, dec_x=None):
    pieces, chunks, weight_parts = len(xs), len(weights), len(weights[0])
    rows, width = xs[1].shape
    span = rows * pieces
    columns = weights[0][0].shape[-1]
    with_decode = dec_x is not None
    out_shape = [jax.ShapeDtypeStruct((span, chunks * 128), BF16)]
    out_specs = [pl.BlockSpec((rows, chunks * 128), lambda g, m: (g, 0))]
    whole = lambda shape: pl.BlockSpec(shape, lambda g, m: (0,) * len(shape))
    in_specs = (
        [ANY] * (pieces + chunks * weight_parts)
        + [whole(gain.shape), whole(table.shape), whole(variates.shape)]
    )
    operands = list(xs) + [part for parts in weights for part in parts] + [gain, table, variates]
    if with_decode:
        in_specs.append(whole(dec_x.shape))
        operands.append(dec_x)
        out_shape.append(jax.ShapeDtypeStruct((chunks, dec_x.shape[0], columns), BF16))
        out_specs.append(whole(out_shape[1].shape))
    req_blocks = weights[0][0].shape[0] * weight_parts
    flops = 2 * span * width * columns * chunks + 2 * chunks * 4 * span * span * 128
    return pl.pallas_call(
        functools.partial(
            attention_kernel,
            pieces=pieces,
            chunks=chunks,
            weight_parts=weight_parts,
            own_slot=own_slot,
            with_decode=with_decode,
        ),
        out_shape=out_shape,
        grid_spec=pltpu.PrefetchScalarGridSpec(
            num_scalar_prefetch=1,
            grid=(pieces,),
            in_specs=in_specs,
            out_specs=out_specs,
            scratch_shapes=[
                pltpu.VMEM((2, rows, width), BF16),
                pltpu.VMEM((chunks, width, columns), BF16),
                pltpu.VMEM((2 * chunks, span, 128), BF16),
                pltpu.VMEM((2 * chunks, span, 128), BF16),
                pltpu.VMEM((span, 128), BF16),
                pltpu.SemaphoreType.DMA((2,)),
                pltpu.SemaphoreType.DMA((chunks, req_blocks)),
            ],
        ),
        compiler_params=pltpu.CompilerParams(vmem_limit_bytes=56 * 2**20),
        cost_estimate=pl.CostEstimate(
            flops=flops, bytes_accessed=span * width * 2, transcendentals=chunks * span * span
        ),
        name="prefill",
    )(meta, *operands)


def decode_kernel(meta, qkv_ref, bias_ref, cache_ref, prompt_ref, cache_var_ref, prompt_var_ref, out_ref):
    request = pl.program_id(0)
    requests = pl.num_programs(0)
    fsdp_index = meta[0]
    length, variate = meta[1 + request], meta[1 + requests + request]
    width = qkv_ref.shape[-1]
    heads = bias_ref.shape[1]
    size = width // heads
    own_head = lax.broadcasted_iota(jnp.int32, (heads, width), 1) // size == lax.broadcasted_iota(
        jnp.int32, (heads, width), 0
    )
    query = qkv_ref[0, 0:1, :].astype(F32)
    spread = jnp.where(own_head, query, 0.0)
    spread_low = spread.astype(BF16)
    same_bias, diff_bias = bias_ref[0], bias_ref[1]
    scaling = 1.0 / math.sqrt(size)

    def scores(kv_ref, var_ref):
        raw = lax.dot_general(spread_low, kv_ref[0, :, :width], NT, preferred_element_type=F32)
        return raw * scaling + jnp.where(var_ref[0] == variate, same_bias, diff_bias)

    cache_rows = cache_ref.shape[1]
    cache_scores = scores(cache_ref, cache_var_ref)
    spot = fsdp_index * cache_rows + lax.broadcasted_iota(jnp.int32, (1, cache_rows), 1)
    valid = spot < length
    cache_scores = jnp.where(valid, cache_scores, big_negative)
    prompt_scores = scores(prompt_ref, prompt_var_ref)
    own_score = (
        jnp.sum(spread * qkv_ref[0, 1:2, :].astype(F32), axis=1, keepdims=True) * scaling + same_bias
    )
    own_score = jnp.where(fsdp_index == 0, own_score, big_negative)
    top = jnp.maximum(
        jnp.maximum(
            jnp.max(cache_scores, axis=1, keepdims=True), jnp.max(prompt_scores, axis=1, keepdims=True)
        ),
        own_score,
    )
    cache_weights = jnp.where(valid, jnp.exp(cache_scores - top), 0.0)
    prompt_weights = jnp.exp(prompt_scores - top)
    own_weight = jnp.where(fsdp_index == 0, jnp.exp(own_score - top), 0.0)
    total = (
        jnp.sum(cache_weights, axis=1, keepdims=True)
        + jnp.sum(prompt_weights, axis=1, keepdims=True)
        + own_weight
    )
    mixed = jnp.dot(cache_weights.astype(BF16), cache_ref[0, :, width:], preferred_element_type=F32)
    mixed = mixed + jnp.dot(
        prompt_weights.astype(BF16), prompt_ref[0, :, width:], preferred_element_type=F32
    )
    mixed = mixed + own_weight.astype(BF16).astype(F32) * qkv_ref[0, 2:3, :].astype(F32)

    def pick(part):
        return jnp.sum(jnp.where(own_head, part, 0.0), axis=0, keepdims=True)

    out_ref[0] = jnp.concatenate([pick(mixed), pick(top), pick(total)], axis=0)


def decode(meta, groups, qkv, bias, cache_kv, prompt_kv, cache_variate, prompt_variate):
    requests, cache_rows, both = cache_kv.shape
    prompt_rows = prompt_kv.shape[1]
    width = both // 2
    own = lambda shape: pl.BlockSpec((1,) + shape, lambda r, m, g: (r, 0, 0))
    shared = lambda shape: pl.BlockSpec((1,) + shape, lambda r, m, g: (g[r], 0, 0))
    return pl.pallas_call(
        lambda m, g, *refs: decode_kernel(m, *refs),
        out_shape=jax.ShapeDtypeStruct((requests, 3, width), F32),
        grid_spec=pltpu.PrefetchScalarGridSpec(
            num_scalar_prefetch=2,
            grid=(requests,),
            in_specs=[
                own((3, width)),
                pl.BlockSpec(bias.shape, lambda r, m, g: (0, 0, 0)),
                own((cache_rows, both)),
                shared((prompt_rows, both)),
                own((1, cache_rows)),
                shared((1, prompt_rows)),
            ],
            out_specs=own((3, width)),
        ),
        compiler_params=pltpu.CompilerParams(vmem_limit_bytes=48 * 2**20),
        cost_estimate=pl.CostEstimate(
            flops=4 * requests * (cache_rows + prompt_rows) * width * 16,
            bytes_accessed=(cache_kv.size + requests * prompt_rows * both) * 2,
            transcendentals=0,
        ),
        name="decode",
    )(
        meta,
        groups,
        qkv,
        bias,
        cache_kv,
        prompt_kv,
        cache_variate.reshape(requests, 1, cache_rows),
        prompt_variate.reshape(prompt_variate.shape[0], 1, prompt_rows),
    )


def out_kernel(meta, *refs, sources, chunk_list, weight_parts, components):
    refs = list(refs)
    x_ref = refs.pop(0)
    runs = len(chunk_list)
    attn = [[[refs.pop(0) for _ in range(sources)] for _ in calls] for calls in chunk_list]
    weights = [[refs.pop(0) for _ in range(weight_parts)] for _ in range(2)]
    dec_x_ref, parts_ref = refs.pop(0), refs.pop(0)
    out_ref, fore_ref, dec_out_ref, dec_fore_ref = (refs.pop(0) for _ in range(4))
    abuf, wbuf, asems, wsems = refs
    fsdp_index, req_index = meta[0], meta[1]
    step = pl.program_id(0)
    rows, width = x_ref.shape[1:]
    own_width = width // sources
    w_rows = wbuf.shape[1] // (weights[0][0].shape[0] * weight_parts)

    def w_copies():
        copies = []
        for i in range(2):
            target = wbuf.at[(fsdp_index & 1) ^ i]
            copies += weight_copies(weights[i], target, wsems.at[i], req_index, w_rows)
        return copies

    def a_copies(run):
        copies = []
        for call, (first, size) in enumerate(chunk_list[run]):
            for j in range(sources):
                source = attn[run][call][j]
                if j == 0:
                    source = source.at[pl.ds(pl.multiple_of(fsdp_index * rows, rows), rows)]
                column = pl.multiple_of((fsdp_index ^ j) * own_width + first, 128)
                copies.append(
                    pltpu.make_async_copy(
                        source, abuf.at[run, :, pl.ds(column, size)], asems.at[run, call, j]
                    )
                )
        return copies

    half = wbuf.shape[2]

    def finish(rows_in, mixed_in):
        left = jnp.dot(mixed_in, wbuf[0], preferred_element_type=F32)
        right = jnp.dot(mixed_in, wbuf[1, :, : width - half], preferred_element_type=F32)
        result = (rows_in.astype(F32) + jnp.concatenate([left, right], axis=1)).astype(BF16)
        scaled = normalise(result, None)
        both = jnp.dot(scaled, wbuf[1, :, width - half :], preferred_element_type=F32)
        centers, logits = both[:, :128], both[:, 128:]
        group = 128 // components

        def around(part, join):
            shift = group
            while shift < 128:
                part = join(part, pltpu.roll(part, shift, 1))
                shift *= 2
            return part

        weights_mix = jnp.exp(logits - around(logits, jnp.maximum))
        share = weights_mix / around(weights_mix, jnp.add)
        return result, around(share * centers, jnp.add)[:, :group]

    @pl.when(step == 0)
    def _():
        for copy in w_copies():
            copy.start()
        for run in range(runs):
            for copy in a_copies(run):
                copy.start()
        for copy in w_copies():
            copy.wait()
        parts = parts_ref[...]
        top = parts[0, 1]
        for i in range(1, sources):
            top = jnp.maximum(top, parts[i, 1])
        total = jnp.zeros_like(top)
        mixed = jnp.zeros_like(top)
        for i in range(sources):
            factor = jnp.exp(parts[i, 1] - top)
            total = total + parts[i, 2] * factor
            mixed = mixed + parts[i, 0] * factor
        result, fore = finish(dec_x_ref[...], (mixed / total).astype(BF16))
        dec_out_ref[...] = result
        dec_fore_ref[...] = fore

    for run in range(runs):

        @pl.when(step == run)
        def _(run=run):
            for copy in a_copies(run):
                copy.wait()
            result, fore = finish(x_ref[0], abuf[run])
            out_ref[0] = result
            fore_ref[0] = fore


def finish_rows(meta, stretch_x, attn, chunk_list, weights, dec_x, parts, components):
    runs, rows, width = stretch_x.shape
    sources = parts.shape[0]
    weight_parts = len(weights[0])
    group = 128 // components
    flat = [part for calls in attn for call in calls for part in call]
    flat_weights = [part for parts_of in weights for part in parts_of]
    half = flat_weights[0].shape[-1]
    req_blocks = flat_weights[0].shape[0] * weight_parts
    whole = lambda shape: pl.BlockSpec(shape, lambda g, m: (0,) * len(shape))
    return pl.pallas_call(
        functools.partial(
            out_kernel,
            sources=sources,
            chunk_list=chunk_list,
            weight_parts=weight_parts,
            components=components,
        ),
        out_shape=[
            jax.ShapeDtypeStruct((runs, rows, width), BF16),
            jax.ShapeDtypeStruct((runs, rows, group), F32),
            jax.ShapeDtypeStruct(dec_x.shape, BF16),
            jax.ShapeDtypeStruct((dec_x.shape[0], group), F32),
        ],
        grid_spec=pltpu.PrefetchScalarGridSpec(
            num_scalar_prefetch=1,
            grid=(runs,),
            in_specs=[pl.BlockSpec((1, rows, width), lambda g, m: (g, 0, 0))]
            + [ANY] * (len(flat) + len(flat_weights))
            + [whole(dec_x.shape), whole(parts.shape)],
            out_specs=[
                pl.BlockSpec((1, rows, width), lambda g, m: (g, 0, 0)),
                pl.BlockSpec((1, rows, group), lambda g, m: (g, 0, 0)),
                whole(dec_x.shape),
                whole((dec_x.shape[0], group)),
            ],
            scratch_shapes=[
                pltpu.VMEM((runs, rows, width), BF16),
                pltpu.VMEM((2, width, half), BF16),
                pltpu.SemaphoreType.DMA((runs, max(len(calls) for calls in chunk_list), sources)),
                pltpu.SemaphoreType.DMA((2, req_blocks)),
            ],
        ),
        compiler_params=pltpu.CompilerParams(vmem_limit_bytes=48 * 2**20),
        cost_estimate=pl.CostEstimate(
            flops=2 * runs * rows * width * (width + 256),
            bytes_accessed=3 * runs * rows * width * 2,
            transcendentals=0,
        ),
        name="finish",
    )(meta, stretch_x, *flat, *flat_weights, dec_x, parts)


def bias_table(bias_same, bias_diff):
    both = jnp.stack([bias_same, bias_diff], axis=1) * log2e
    terms = []
    rest = both
    for _ in range(3):
        term = lax.reduce_precision(rest, 8, 7)
        terms.append(term)
        rest = rest - term
    lanes = jnp.repeat(jnp.stack(terms, axis=-1), 4, axis=-1)
    ones = jnp.ones(both.shape + (1,), F32)
    zeros = jnp.zeros(both.shape + (115,), F32)
    return jnp.concatenate([lanes, ones, zeros], axis=-1)


def shards(
    stretch_x,
    dec_x,
    w_qkv,
    w_out,
    w_loc,
    w_mix,
    attn_gain,
    bias_same,
    bias_diff,
    cache_kv,
    prompt_kv,
    stretch_len,
    cache_len,
    prompt_group,
    pre_variate,
    dec_variate,
    cache_variate,
    prompt_variate,
    *,
    req_size,
    fsdp_size,
):
    runs, rows, width = stretch_x.shape
    decodes = dec_x.shape[0]
    heads = bias_same.shape[0]
    components = w_mix.shape[1]
    fsdp_index = lax.axis_index("fsdp").astype(jnp.int32)
    req_index = lax.axis_index("req").astype(jnp.int32)
    own_heads = heads // fsdp_size
    own_width = width // fsdp_size
    chunks = own_width // 128

    def gather_rows(own):
        got = {0: own}
        offset = fsdp_size // 2
        while offset:
            got.update({j | offset: swap(part, "fsdp", fsdp_size, offset) for j, part in list(got.items())})
            offset //= 2
        return [got[j] for j in range(fsdp_size)]

    x_pieces = [gather_rows(stretch_x[s]) for s in range(runs)]

    w_rows = w_qkv.shape[0]
    per_device = w_qkv.reshape(w_rows, 3, fsdp_size, chunks, 128)
    per_device = jnp.transpose(per_device, (2, 0, 3, 1, 4)).reshape(fsdp_size, w_rows, chunks * 384)
    others = jnp.concatenate([w_out, w_loc, jnp.repeat(w_mix, 128 // components, axis=1)], axis=1)
    half = others.shape[1] // 2
    others = jnp.transpose(others.reshape(w_rows, 2, half), (1, 0, 2))
    others = jnp.tile(others, (fsdp_size // 2, 1, 1))
    sent = jnp.concatenate([per_device, others], axis=2)
    sent = lax.all_to_all(sent, "fsdp", 0, 0, tiled=True)
    sent = sent.reshape(fsdp_size * w_rows, -1)

    def gather_weight(piece):
        got = jnp.stack([piece] + [swap(piece, "req", req_size, j) for j in range(2, req_size, 2)])
        return [got, swap(got, "req", req_size, 1)]

    w_chunks = [gather_weight(sent[:, n * 384 : (n + 1) * 384]) for n in range(chunks)]
    w_own = gather_weight(sent[:, chunks * 384 :])
    w_other = [swap(part, "fsdp", fsdp_size, 1) for part in w_own]

    gain = attn_gain.reshape(1, width)
    table = bias_table(bias_same, bias_diff)
    table = lax.dynamic_slice_in_dim(table, fsdp_index * own_heads, own_heads, 0)

    def call(run, which, with_decode):
        meta = jnp.stack([fsdp_index, req_index, stretch_len[run]])
        xs = [stretch_x] + x_pieces[run][1:]
        return attention(
            meta,
            xs,
            run,
            [w_chunks[n] for n in which],
            gain,
            table[2 * which[0] : 2 * which[-1] + 2],
            pre_variate[run : run + 1],
            dec_x if with_decode else None,
        )

    attn, chunk_list, dec_parts = [], [], []

    def give_back(whole_rows):
        return [whole_rows] + [
            swap(
                lax.dynamic_slice_in_dim(whole_rows, (fsdp_index ^ j) * rows, rows, 0),
                "fsdp",
                fsdp_size,
                j,
            )
            for j in range(1, fsdp_size)
        ]

    for run in range(runs):
        groups = [[n] for n in range(chunks)] if run == 0 else [list(range(chunks))]
        attn.append([])
        chunk_list.append([])
        for which in groups:
            result = call(run, which, run == 0)
            attn[run].append(give_back(result[0]))
            chunk_list[run].append((which[0] * 128, len(which) * 128))
            if run == 0:
                dec_parts.append(result[1])

    dec_own = jnp.concatenate(dec_parts, axis=0)
    dec_all = lax.all_gather(dec_own, "fsdp")
    dec_all = dec_all.reshape(fsdp_size, chunks, decodes, 3, 128)
    dec_qkv = jnp.transpose(dec_all, (2, 3, 0, 1, 4)).reshape(decodes, 3, width)
    dec_meta = jnp.concatenate([fsdp_index[None], cache_len, dec_variate])
    bias = jnp.stack([bias_same, bias_diff])[:, :, None]
    partial = decode(
        dec_meta, prompt_group, dec_qkv, bias, cache_kv, prompt_kv, cache_variate, prompt_variate
    )
    parts = lax.all_gather(jnp.transpose(partial, (1, 0, 2)), "fsdp")

    meta = jnp.stack([fsdp_index, req_index])
    pre_out, pre_fore, dec_out, dec_fore = finish_rows(
        meta, stretch_x, attn, chunk_list, [w_own, w_other], dec_x, parts, components
    )
    return pre_out, dec_out, pre_fore, dec_fore


def solution(mesh):
    return jax.shard_map(
        functools.partial(shards, req_size=mesh.shape["req"], fsdp_size=mesh.shape["fsdp"]),
        mesh=mesh,
        in_specs=(
            P("req", "fsdp", None),
            P("req", None),
            P(("req", "fsdp"), None),
            P(("req", "fsdp"), None),
            P(("req", "fsdp"), None),
            P(("req", "fsdp"), None),
            P(),
            P(),
            P(),
            P("req", "fsdp", None),
            P(None, "fsdp", None),
            P("req"),
            P("req"),
            P("req"),
            P("req", None),
            P("req"),
            P("req", "fsdp"),
            P(None, "fsdp"),
        ),
        out_specs=(P("req", "fsdp", None), P("req", None), P("req", "fsdp", None), P("req", None)),
        check_vma=False,
    )
```

```python
import functools
import math

import jax
import jax.numpy as jnp
from jax import lax
from jax.experimental import pallas as pl
from jax.experimental.pallas import tpu as pltpu
from jax.sharding import PartitionSpec as P

epsilon = 1e-05
big_negative = -1e30
log2e = math.log2(math.e)
F32 = jnp.float32
BF16 = jnp.bfloat16
ANY = pl.BlockSpec(memory_space=pl.ANY)
VMEM = pl.BlockSpec(memory_space=pltpu.VMEM)
NT = (((1,), (1,)), ((), ()))


def swap(value, axis, size, offset):
    return lax.ppermute(value, axis, [(i, i ^ offset) for i in range(size)])


def normalise(rows, gain):
    as_float = rows.astype(F32)
    factor = lax.rsqrt(jnp.mean(as_float * as_float, axis=-1, keepdims=True) + epsilon)
    scaled = as_float * factor
    return (scaled if gain is None else scaled * gain).astype(BF16)


def weight_copies(pieces, target, sems, req_index):
    copies = []
    for j, piece in enumerate(pieces):
        rows = piece.shape[0]
        first = pl.multiple_of((req_index ^ j) * rows, rows)
        copies.append(pltpu.make_async_copy(piece, target.at[pl.ds(first, rows)], sems.at[j]))
    return copies


def prepare_kernel(qkv_ref, out_ref, loc_ref, mix_ref, sent_ref):
    devices = sent_ref.shape[0]
    width = out_ref.shape[1]
    own = width // devices
    half = sent_ref.shape[2] - 3 * own
    components = mix_ref.shape[0]
    pick = lax.broadcasted_iota(jnp.int32, (components, 128), 1) // (
        128 // components
    ) == lax.broadcasted_iota(jnp.int32, (components, 128), 0)
    mix = lax.dot_general(
        mix_ref[...], pick.astype(BF16), (((0,), (0,)), ((), ())), preferred_element_type=F32
    )
    for device in range(devices):
        for n in range(own // 128):
            for part in range(3):
                source = part * width + device * own + n * 128
                target = (3 * n + part) * 128
                sent_ref[device, :, target : target + 128] = qkv_ref[:, source : source + 128]
        if device % 2 == 0:
            sent_ref[device, :, 3 * own :] = out_ref[:, :half]
        else:
            rest = 3 * own + width - half
            sent_ref[device, :, 3 * own : rest] = out_ref[:, half:]
            sent_ref[device, :, rest : rest + 128] = loc_ref[...]
            sent_ref[device, :, rest + 128 :] = mix.astype(BF16)


def prepare(w_qkv, w_out, w_loc, w_mix, devices):
    rows, width = w_out.shape
    columns = 3 * width // devices + (width + 256) // 2
    return pl.pallas_call(
        prepare_kernel,
        out_shape=jax.ShapeDtypeStruct((devices, rows, columns), BF16),
        name="prepare",
    )(w_qkv, w_out, w_loc, w_mix.T)


def attention_kernel(meta, *refs, pieces, weight_parts, own_slot, with_decode):
    refs = list(refs)
    xs = [refs.pop(0) for _ in range(pieces)]
    weights = [refs.pop(0) for _ in range(weight_parts)]
    gain_ref, table_ref, variate_ref = refs.pop(0), refs.pop(0), refs.pop(0)
    dec_ref = refs.pop(0) if with_decode else None
    outs = [refs.pop(0) for _ in range(pieces)]
    xbuf, wbuf, keys, values, key_extra, queries, held, obuf, xsems, wsems, osems = refs
    chunks = keys.shape[0] // 2
    fsdp_index, req_index, length = meta[0], meta[1], meta[2 + own_slot]
    block = pl.program_id(0)
    rows = xbuf.shape[1]
    tile = math.gcd(rows, 256)
    splits = 4
    per_step = 4
    part = rows // splits

    def fetch_part(source, slot, i):
        here = pl.ds(i * part, part)
        return pltpu.make_async_copy(source.at[here], xbuf.at[slot, here], xsems.at[slot, i])

    def fetch(which, slot):
        offset = which ^ fsdp_index
        for j in range(pieces):
            source = xs[j].at[own_slot] if j == 0 else xs[j]

            @pl.when(offset == j)
            def _():
                for i in range(splits):
                    fetch_part(source, slot, i).start()

    slot = lax.rem(block, 2)

    @pl.when(block == 0)
    def _():
        fetch(block, slot)
        for copy in weight_copies(weights, wbuf, wsems, req_index):
            copy.start()

    @pl.when(block + 1 < pieces)
    def _():
        fetch(block + 1, 1 - slot)

    for i in range(splits):
        fetch_part(xs[0].at[own_slot], slot, i).wait()
    normed = normalise(xbuf[slot], gain_ref[...])
    first_row = pl.multiple_of(block * rows, rows)
    here = pl.ds(first_row, rows)
    lane = lax.broadcasted_iota(jnp.int32, (rows, 128), 1)
    low = lane < 64
    variate = jnp.broadcast_to(variate_ref[:, here].astype(F32), (128, rows)).T.astype(jnp.int32)
    same = (lane & 3) == variate
    position = first_row + lax.broadcasted_iota(jnp.int32, (rows, 128), 0)
    extra = jnp.where(
        lane < 12,
        jnp.where(same, 1.0, 0.0),
        jnp.where((lane == 12) & (position >= length), big_negative, 0.0),
    )
    key_extra[here, :] = extra.astype(BF16)

    @pl.when(block == 0)
    def _():
        for copy in weight_copies(weights, wbuf, wsems, req_index):
            copy.wait()
        if with_decode:
            dec_rows = normalise(dec_ref[...], gain_ref[...])
            dec_qkv = jnp.dot(dec_rows, wbuf[...], preferred_element_type=F32).astype(BF16)
            padded = dec_ref.shape[0]
            for i in range(pieces):
                for n in range(chunks):
                    for which in range(3):
                        first = rows + which * padded
                        source = (3 * n + which) * 128
                        obuf[i, first : first + padded, n * 128 : (n + 1) * 128] = dec_qkv[
                            :, source : source + 128
                        ]

    everything = jnp.dot(normed, wbuf[...], preferred_element_type=F32)
    for n in range(chunks):
        projected = everything[:, n * 384 : (n + 1) * 384].astype(BF16)
        q = projected[:, :128].astype(F32) * (log2e * 0.125)
        k = projected[:, 128:256].astype(F32)
        v = projected[:, 256:].astype(F32)
        q_high = q.astype(BF16).astype(F32)
        q_low = q - q_high
        q_high_turned = pltpu.roll(q_high, 64, 1)
        q_low_turned = pltpu.roll(q_low, 64, 1)
        k_turned = pltpu.roll(k, 64, 1)
        keys[2 * n, here, :] = jnp.where(low, k, k_turned).astype(BF16)
        keys[2 * n + 1, here, :] = jnp.where(low, k_turned, k).astype(BF16)
        values[2 * n, here, :] = jnp.where(low, v, 1.0).astype(BF16)
        values[2 * n + 1, here, :] = jnp.where(low, 1.0, v).astype(BF16)
        for half, q_main in (
            (0, jnp.where(low, q_high, q_low_turned)),
            (1, jnp.where(low, q_high_turned, q_low)),
        ):
            bias = table_ref[2 * n + half]
            q_extra = jnp.where(same, bias[0:1], bias[1:2])
            queries[2 * n + half, :, :128] = q_main.astype(BF16)
            queries[2 * n + half, :, 128:] = q_extra.astype(BF16)

    for c in range(pieces):

        @pl.when(block == c)
        def _(c=c):
            diagonal = lax.broadcasted_iota(jnp.int32, (tile, tile), 1) <= lax.broadcasted_iota(
                jnp.int32, (tile, tile), 0
            )
            def score(head, t):
                span = c * rows + (t + 1) * tile
                query = queries[head, t * tile : (t + 1) * tile, :]
                result = []
                for first, last in ((0, span - tile), (span - tile, span)):
                    if first < last:
                        key = jnp.concatenate(
                            [keys[head, first:last, :], key_extra[first:last, :]], axis=1
                        )
                        result.append(
                            lax.dot_general(query, key, NT, preferred_element_type=F32)
                        )
                result[-1] = jnp.where(diagonal, result[-1], big_negative)
                return result

            def mix(head, t, scores):
                top = functools.reduce(
                    jnp.maximum, [jnp.max(part, axis=1, keepdims=True) for part in scores]
                )
                total, first = 0.0, 0
                for part in scores:
                    last = first + part.shape[1]
                    total = total + jnp.dot(
                        jnp.exp2(part - top).astype(BF16),
                        values[head, first:last, :],
                        preferred_element_type=F32,
                    )
                    first = last
                mixed = total / pltpu.roll(total, 64, 1)
                held[head, t * tile : (t + 1) * tile, :] = mixed.astype(BF16)

            def some_heads(step, carry):
                units = [
                    (step * per_step + i, t) for i in range(per_step) for t in range(rows // tile)
                ]
                ready = score(*units[0])
                for i, unit in enumerate(units):
                    current = ready
                    if i + 1 < len(units):
                        ready = score(*units[i + 1])
                    mix(*unit, current)
                return carry

            lax.fori_loop(0, 2 * chunks // per_step, some_heads, 0)

    for n in range(chunks):
        obuf[block, :rows, n * 128 : (n + 1) * 128] = jnp.where(low, held[2 * n], held[2 * n + 1])
    for j in range(pieces):

        @pl.when(fsdp_index ^ block == j)
        def _(j=j):
            pltpu.make_async_copy(obuf.at[block], outs[j], osems.at[block]).start()

    @pl.when(block + 1 == pieces)
    def _():
        for i in range(pieces):
            pltpu.make_async_copy(obuf.at[i], outs[0], osems.at[i]).wait()


def attention(meta, xs, own_slot, weights, gain, table, variates, dec_x=None):
    pieces, weight_parts = len(xs), len(weights)
    rows, width = xs[1].shape
    span = rows * pieces
    columns = weights[0].shape[-1]
    chunks = columns // 384
    with_decode = dec_x is not None
    whole = lambda shape: pl.BlockSpec(shape, lambda g, m: (0,) * len(shape))
    out_rows = rows + (3 * dec_x.shape[0] if with_decode else 0)
    out_shape = [jax.ShapeDtypeStruct((out_rows, chunks * 128), BF16)] * pieces
    out_specs = [ANY] * pieces
    in_specs = [ANY] * (pieces + weight_parts) + [
        whole(gain.shape),
        whole(table.shape),
        whole(variates.shape),
    ]
    operands = list(xs) + list(weights) + [gain, table, variates]
    if with_decode:
        in_specs.append(whole(dec_x.shape))
        operands.append(dec_x)
    flops = 2 * span * width * columns + 2 * chunks * 4 * span * span * 128
    return pl.pallas_call(
        functools.partial(
            attention_kernel,
            pieces=pieces,
            weight_parts=weight_parts,
            own_slot=own_slot,
            with_decode=with_decode,
        ),
        out_shape=out_shape,
        grid_spec=pltpu.PrefetchScalarGridSpec(
            num_scalar_prefetch=1,
            grid=(pieces,),
            in_specs=in_specs,
            out_specs=out_specs,
            scratch_shapes=[
                pltpu.VMEM((2, rows, width), BF16),
                pltpu.VMEM((width, columns), BF16),
                pltpu.VMEM((2 * chunks, span, 128), BF16),
                pltpu.VMEM((2 * chunks, span, 128), BF16),
                pltpu.VMEM((span, 128), BF16),
                pltpu.VMEM((2 * chunks, rows, 256), BF16),
                pltpu.VMEM((2 * chunks, rows, 128), BF16),
                pltpu.VMEM((pieces, out_rows, chunks * 128), BF16),
                pltpu.SemaphoreType.DMA((2, 4)),
                pltpu.SemaphoreType.DMA((weight_parts,)),
                pltpu.SemaphoreType.DMA((pieces,)),
            ],
        ),
        compiler_params=pltpu.CompilerParams(vmem_limit_bytes=60 * 2**20),
        cost_estimate=pl.CostEstimate(
            flops=flops, bytes_accessed=span * width * 2, transcendentals=chunks * span * span
        ),
        name="prefill",
    )(meta, *operands)


def decode_kernel(meta, groups, lengths, variates, *refs, sources, first_row):
    qkv_refs, refs = refs[:sources], refs[sources:]
    same_ref, diff_ref, cache_ref, prompt_ref, cache_var_ref, prompt_var_ref, out_ref = refs[:7]
    got, held, sems = refs[7:]
    request = pl.program_id(0)
    fsdp_index = meta[0]
    length, variate = lengths[request], variates[request]
    width = out_ref.shape[-1]
    heads = same_ref.shape[1]
    size = width // heads
    own_width = width // sources
    padded = held.shape[1]

    @pl.when(request == 0)
    def _():
        copies = [
            pltpu.make_async_copy(
                qkv_refs[j].at[pl.ds(first_row, 3 * padded)], got.at[j], sems.at[j]
            )
            for j in range(sources)
        ]
        for copy in copies:
            copy.start()
        for copy in copies:
            copy.wait()
        for j in range(sources):
            for n in range(own_width // 128):
                for which in range(3):
                    column = pl.multiple_of((fsdp_index ^ j) * own_width + n * 128, 128)
                    part = got[j, which * padded : (which + 1) * padded, n * 128 : (n + 1) * 128]
                    held[which, :, pl.ds(column, 128)] = part.astype(F32)

    corner = lax.broadcasted_iota(jnp.int32, (heads, heads), 0) == lax.broadcasted_iota(
        jnp.int32, (heads, heads), 1
    )
    same_bias = jnp.sum(jnp.where(corner, same_ref[...], 0.0), axis=1, keepdims=True)
    diff_bias = jnp.sum(jnp.where(corner, diff_ref[...], 0.0), axis=1, keepdims=True)
    own_head = lax.broadcasted_iota(jnp.int32, (heads, width), 1) // size == lax.broadcasted_iota(
        jnp.int32, (heads, width), 0
    )
    row = pl.ds(request, 1)
    query, own_key, own_value = held[0, row, :], held[1, row, :], held[2, row, :]
    spread = jnp.where(own_head, query, 0.0)
    spread_low = spread.astype(BF16)
    scaling = 1.0 / math.sqrt(size)

    def scores(kv_ref, key_variates):
        raw = lax.dot_general(spread_low, kv_ref[0, :, :width], NT, preferred_element_type=F32)
        return raw * scaling + jnp.where(key_variates == variate, same_bias, diff_bias)

    cache_rows = cache_ref.shape[1]
    cache_scores = scores(cache_ref, cache_var_ref[pl.ds(request, 1), :])
    spot = fsdp_index * cache_rows + lax.broadcasted_iota(jnp.int32, (1, cache_rows), 1)
    valid = spot < length
    cache_scores = jnp.where(valid, cache_scores, big_negative)
    prompt_scores = scores(prompt_ref, prompt_var_ref[pl.ds(groups[request], 1), :])
    own_score = (
        jnp.sum(spread * own_key, axis=1, keepdims=True) * scaling + same_bias
    )
    own_score = jnp.where(fsdp_index == 0, own_score, big_negative)
    top = jnp.maximum(
        jnp.maximum(
            jnp.max(cache_scores, axis=1, keepdims=True), jnp.max(prompt_scores, axis=1, keepdims=True)
        ),
        own_score,
    )
    cache_weights = jnp.where(valid, jnp.exp(cache_scores - top), 0.0)
    prompt_weights = jnp.exp(prompt_scores - top)
    own_weight = jnp.where(fsdp_index == 0, jnp.exp(own_score - top), 0.0)
    total = (
        jnp.sum(cache_weights, axis=1, keepdims=True)
        + jnp.sum(prompt_weights, axis=1, keepdims=True)
        + own_weight
    )
    mixed = jnp.dot(cache_weights.astype(BF16), cache_ref[0, :, width:], preferred_element_type=F32)
    mixed = mixed + jnp.dot(
        prompt_weights.astype(BF16), prompt_ref[0, :, width:], preferred_element_type=F32
    )
    mixed = mixed + own_weight.astype(BF16).astype(F32) * own_value

    def pick(part):
        return jnp.sum(jnp.where(own_head, part, 0.0), axis=0, keepdims=True)

    out_ref[0, row, :] = pick(mixed)
    out_ref[1, row, :] = pick(top)
    out_ref[2, row, :] = pick(total)


def decode(
    meta, groups, lengths, variates, qkv, first_row, padded, biases, cache_kv, prompt_kv, key_variates
):
    requests, cache_rows, both = cache_kv.shape
    prompt_rows = prompt_kv.shape[1]
    width = both // 2
    sources = len(qkv)
    whole = lambda array: pl.BlockSpec(array.shape, lambda r, *s: (0,) * array.ndim)
    return pl.pallas_call(
        functools.partial(decode_kernel, sources=sources, first_row=first_row),
        out_shape=jax.ShapeDtypeStruct((3, requests, width), F32),
        grid_spec=pltpu.PrefetchScalarGridSpec(
            num_scalar_prefetch=4,
            grid=(requests,),
            in_specs=[ANY] * sources
            + [whole(bias) for bias in biases]
            + [
                pl.BlockSpec((1, cache_rows, both), lambda r, *s: (r, 0, 0)),
                pl.BlockSpec((1, prompt_rows, both), lambda r, m, g, *s: (g[r], 0, 0)),
            ]
            + [whole(ids) for ids in key_variates],
            out_specs=pl.BlockSpec((3, requests, width), lambda r, *s: (0, 0, 0)),
            scratch_shapes=[
                pltpu.VMEM((sources, 3 * padded, width // sources), BF16),
                pltpu.VMEM((3, padded, width), F32),
                pltpu.SemaphoreType.DMA((sources,)),
            ],
        ),
        compiler_params=pltpu.CompilerParams(vmem_limit_bytes=60 * 2**20),
        cost_estimate=pl.CostEstimate(
            flops=4 * requests * (cache_rows + prompt_rows) * width * 16,
            bytes_accessed=(cache_kv.size + requests * prompt_rows * both) * 2,
            transcendentals=0,
        ),
        name="decode",
    )(meta, groups, lengths, variates, *qkv, *biases, cache_kv, prompt_kv, *key_variates)


def out_kernel(meta, *refs, sources, weight_parts, components, with_decode, aliased):
    refs = list(refs)
    x_ref = refs.pop(0)
    attn = [refs.pop(0) for _ in range(sources)]
    weights = [[refs.pop(0) for _ in range(weight_parts)] for _ in range(2)]
    if with_decode:
        dec_x_ref = refs.pop(0)
        parts = [refs.pop(0) for _ in range(sources)]
    refs = refs[aliased:]
    out_ref, fore_ref = refs.pop(0), refs.pop(0)
    if with_decode:
        dec_out_ref, dec_fore_ref = refs.pop(0), refs.pop(0)
    abuf, wbuf, asems, wsems = refs
    fsdp_index, req_index = meta[0], meta[1]
    step = pl.program_id(0)
    tile, width = x_ref.shape[1:]
    own_width = width // sources
    half = wbuf.shape[2]

    def copies():
        result = []
        for i in range(2):
            target = wbuf.at[(fsdp_index & 1) ^ i]
            flat = [piece.at[j] for j in range(weights[i][0].shape[0]) for piece in weights[i]]
            result += weight_copies(flat, target, wsems.at[i], req_index)
        for j in range(sources):
            column = pl.multiple_of((fsdp_index ^ j) * own_width, 128)
            result.append(
                pltpu.make_async_copy(
                    attn[j].at[pl.ds(0, abuf.shape[0])],
                    abuf.at[:, pl.ds(column, own_width)],
                    asems.at[j],
                )
            )
        return result

    def finish(rows_in, mixed_in):
        left = jnp.dot(mixed_in, wbuf[0], preferred_element_type=F32)
        right = jnp.dot(mixed_in, wbuf[1, :, : width - half], preferred_element_type=F32)
        result = (rows_in.astype(F32) + jnp.concatenate([left, right], axis=1)).astype(BF16)
        scaled = normalise(result, None)
        both = jnp.dot(scaled, wbuf[1, :, width - half :], preferred_element_type=F32)
        centers, logits = both[:, :128], both[:, 128:]
        group = 128 // components

        def around(part, join):
            shift = group
            while shift < 128:
                part = join(part, pltpu.roll(part, shift, 1))
                shift *= 2
            return part

        weights_mix = jnp.exp(logits - around(logits, jnp.maximum))
        share = weights_mix / around(weights_mix, jnp.add)
        return result, around(share * centers, jnp.add)[:, :group]

    @pl.when(step == 0)
    def _():
        for copy in copies():
            copy.start()
        for copy in copies():
            copy.wait()
        if with_decode:
            top = functools.reduce(jnp.maximum, [part[1] for part in parts])
            total = jnp.zeros_like(top)
            mixed = jnp.zeros_like(top)
            for part in parts:
                factor = jnp.exp(part[1] - top)
                total = total + part[2] * factor
                mixed = mixed + part[0] * factor
            result, fore = finish(dec_x_ref[...], (mixed / total).astype(BF16))
            dec_out_ref[...] = result
            dec_fore_ref[...] = fore

    here = pl.ds(pl.multiple_of(step * tile, tile), tile)
    result, fore = finish(x_ref[0], abuf[here, :])
    out_ref[0] = result
    fore_ref[0] = fore


def finish_rows(meta, run, stretch_x, attn, weights, components, previous=(), dec_x=None, parts=()):
    runs, rows, width = stretch_x.shape
    sources = len(attn)
    weight_parts = len(weights[0])
    group = 128 // components
    flat_weights = [part for parts_of in weights for part in parts_of]
    half = flat_weights[0].shape[-1]
    req_blocks = flat_weights[0].shape[0] * weight_parts
    tile = math.gcd(rows, 256)
    whole = lambda shape: pl.BlockSpec(shape, lambda g, m: (0,) * len(shape))
    with_decode = dec_x is not None
    out_shape = [
        jax.ShapeDtypeStruct((runs, rows, width), BF16),
        jax.ShapeDtypeStruct((runs, rows, group), F32),
    ]
    out_specs = [
        pl.BlockSpec((1, tile, width), lambda g, m: (run, g, 0)),
        pl.BlockSpec((1, tile, group), lambda g, m: (run, g, 0)),
    ]
    operands = [stretch_x, *attn, *flat_weights]
    in_specs = [pl.BlockSpec((1, tile, width), lambda g, m: (run, g, 0))] + [ANY] * (len(operands) - 1)
    if with_decode:
        operands += [dec_x, *parts]
        in_specs += [whole(dec_x.shape)] + [whole(part.shape) for part in parts]
        out_shape += [
            jax.ShapeDtypeStruct(dec_x.shape, BF16),
            jax.ShapeDtypeStruct((dec_x.shape[0], group), F32),
        ]
        out_specs += [whole(shape.shape) for shape in out_shape[2:]]
    aliases = {1 + len(operands) + i: i for i in range(len(previous))}
    operands += list(previous)
    in_specs += [ANY] * len(previous)
    return pl.pallas_call(
        functools.partial(
            out_kernel,
            sources=sources,
            weight_parts=weight_parts,
            components=components,
            with_decode=with_decode,
            aliased=len(previous),
        ),
        out_shape=out_shape,
        grid_spec=pltpu.PrefetchScalarGridSpec(
            num_scalar_prefetch=1,
            grid=(rows // tile,),
            in_specs=in_specs,
            out_specs=out_specs,
            scratch_shapes=[
                pltpu.VMEM((rows, width), BF16),
                pltpu.VMEM((2, width, half), BF16),
                pltpu.SemaphoreType.DMA((sources,)),
                pltpu.SemaphoreType.DMA((2, req_blocks)),
            ],
        ),
        input_output_aliases=aliases,
        compiler_params=pltpu.CompilerParams(vmem_limit_bytes=60 * 2**20),
        cost_estimate=pl.CostEstimate(
            flops=2 * rows * width * (width + 256),
            bytes_accessed=3 * rows * width * 2,
            transcendentals=0,
        ),
        name="finish",
    )(meta, *operands)


def bias_table(bias_same, bias_diff):
    both = jnp.stack([bias_same, bias_diff], axis=1) * log2e
    terms = []
    rest = both
    for _ in range(3):
        term = lax.reduce_precision(rest, 8, 7)
        terms.append(term)
        rest = rest - term
    lanes = jnp.repeat(jnp.stack(terms, axis=-1), 4, axis=-1)
    ones = jnp.ones(both.shape + (1,), F32)
    zeros = jnp.zeros(both.shape + (115,), F32)
    return jnp.concatenate([lanes, ones, zeros], axis=-1)


def shards(
    stretch_x,
    dec_x,
    w_qkv,
    w_out,
    w_loc,
    w_mix,
    attn_gain,
    bias_same,
    bias_diff,
    cache_kv,
    prompt_kv,
    stretch_len,
    cache_len,
    prompt_group,
    pre_variate,
    dec_variate,
    cache_variate,
    prompt_variate,
    *,
    req_size,
    fsdp_size,
):
    runs, rows, width = stretch_x.shape
    heads = bias_same.shape[0]
    components = w_mix.shape[1]
    fsdp_index = lax.axis_index("fsdp").astype(jnp.int32)
    req_index = lax.axis_index("req").astype(jnp.int32)
    own_heads = heads // fsdp_size
    own_width = width // fsdp_size
    after = lambda value, *others: lax.optimization_barrier((value,) + others)[0]
    permute = lambda value, offset: swap(value, "fsdp", fsdp_size, offset)

    w_rows = w_qkv.shape[0]
    sent = prepare(w_qkv, w_out, w_loc, w_mix, fsdp_size)
    sent = lax.all_to_all(sent, "fsdp", 0, 0, tiled=True).reshape(fsdp_size * w_rows, -1)
    w_pieces = {0: sent[:, : 3 * own_width]}
    for j in range(2, req_size, 2):
        w_pieces[j] = swap(w_pieces[0], "req", req_size, j)
    for j in range(0, req_size, 2):
        w_pieces[j + 1] = swap(w_pieces[j], "req", req_size, 1)
    w_pieces = [w_pieces[j] for j in range(req_size)]

    def gather_start(own, *others):
        own = after(own, *others)
        return {0: own, fsdp_size // 2: permute(own, fsdp_size // 2)}

    def gather_rest(got):
        offset = fsdp_size // 4
        while offset:
            for j, part in list(got.items()):
                got[j | offset] = permute(part, offset)
            offset //= 2
        return [got[j] for j in range(fsdp_size)]

    x_started = [gather_start(stretch_x[0], sent)]
    for run in range(1, runs):
        x_started.append(gather_start(stretch_x[run], x_started[-1][fsdp_size // 2], *w_pieces))

    gain = attn_gain.reshape(1, width)
    dec_rows = jnp.pad(dec_x, ((0, -dec_x.shape[0] % 16), (0, 0)))
    table = bias_table(bias_same, bias_diff)
    table = lax.dynamic_slice_in_dim(table, fsdp_index * own_heads, own_heads, 0)

    meta = jnp.concatenate([jnp.stack([fsdp_index, req_index]), stretch_len])
    returned = []
    for run in range(runs):
        got = x_started[run]
        wait = attn[:1] if run else w_pieces
        got = {j: after(part, *wait) if j else part for j, part in got.items()}
        x_pieces = gather_rest(got)
        attn = attention(
            meta,
            [stretch_x] + x_pieces[1:],
            run,
            w_pieces,
            gain,
            table,
            pre_variate[run : run + 1],
            dec_rows if run == 0 else None,
        )
        returned.append([attn[0]] + [permute(attn[j], j) for j in range(1, fsdp_size)])
        if run == 0:
            others = after(sent[:, 3 * own_width :], attn[0])
            pair = jnp.stack([others, swap(others, "req", req_size, 1)])

    pairs = [pair] + [swap(pair, "req", req_size, j) for j in range(2, req_size, 2)]
    w_own = jnp.concatenate([after(pairs[0], attn[0])] + pairs[1:], axis=0)
    weights = [[w_own], [permute(w_own, 1)]]

    partial = decode(
        meta,
        after(prompt_group, attn[0]),
        cache_len,
        dec_variate,
        returned[0],
        rows,
        dec_rows.shape[0],
        [bias_same.reshape(1, heads), bias_diff.reshape(1, heads)],
        cache_kv,
        prompt_kv,
        [cache_variate, prompt_variate],
    )
    parts = [partial] + [permute(partial, j) for j in range(1, fsdp_size)]

    returned[0][0] = after(returned[0][0], partial)
    done = ()
    for run in range(runs - 1):
        done = finish_rows(meta, run, stretch_x, returned[run], weights, components, done)
    pre_out, pre_fore, dec_out, dec_fore = finish_rows(
        meta, runs - 1, stretch_x, returned[-1], weights, components, done, dec_x, parts
    )
    return pre_out, dec_out, pre_fore, dec_fore


def solution(mesh):
    return jax.shard_map(
        functools.partial(shards, req_size=mesh.shape["req"], fsdp_size=mesh.shape["fsdp"]),
        mesh=mesh,
        in_specs=(
            P("req", "fsdp", None),
            P("req", None),
            P(("req", "fsdp"), None),
            P(("req", "fsdp"), None),
            P(("req", "fsdp"), None),
            P(("req", "fsdp"), None),
            P(),
            P(),
            P(),
            P("req", "fsdp", None),
            P(None, "fsdp", None),
            P("req"),
            P("req"),
            P("req"),
            P("req", None),
            P("req"),
            P("req", "fsdp"),
            P(None, "fsdp"),
        ),
        out_specs=(P("req", "fsdp", None), P("req", None), P("req", "fsdp", None), P("req", None)),
        check_vma=False,
    )
```

```python
import functools
import math

import jax
import jax.numpy as jnp
from jax import lax
from jax.experimental import pallas as pl
from jax.experimental.pallas import tpu as pltpu
from jax.sharding import PartitionSpec as P

epsilon = 1e-05
big_negative = -1e30
log2e = math.log2(math.e)
F32 = jnp.float32
BF16 = jnp.bfloat16
ANY = pl.BlockSpec(memory_space=pl.ANY)
VMEM = pl.BlockSpec(memory_space=pltpu.VMEM)
NT = (((1,), (1,)), ((), ()))


def swap(value, axis, size, offset):
    return lax.ppermute(value, axis, [(i, i ^ offset) for i in range(size)])


def normalise(rows, gain):
    as_float = rows.astype(F32)
    factor = lax.rsqrt(jnp.mean(as_float * as_float, axis=-1, keepdims=True) + epsilon)
    scaled = as_float * factor
    return (scaled if gain is None else scaled * gain).astype(BF16)


def weight_copies(pieces, target, sems, req_index):
    copies = []
    for j, piece in enumerate(pieces):
        rows = piece.shape[0]
        first = pl.multiple_of((req_index ^ j) * rows, rows)
        copies.append(pltpu.make_async_copy(piece, target.at[pl.ds(first, rows)], sems.at[j]))
    return copies


def prepare_kernel(qkv_ref, out_ref, loc_ref, mix_ref, sent_ref):
    devices = sent_ref.shape[0]
    width = out_ref.shape[1]
    own = width // devices
    half = sent_ref.shape[2] - 3 * own
    components = mix_ref.shape[0]
    pick = lax.broadcasted_iota(jnp.int32, (components, 128), 1) // (
        128 // components
    ) == lax.broadcasted_iota(jnp.int32, (components, 128), 0)
    mix = lax.dot_general(
        mix_ref[...], pick.astype(BF16), (((0,), (0,)), ((), ())), preferred_element_type=F32
    )
    for device in range(devices):
        for n in range(own // 128):
            for part in range(3):
                source = part * width + device * own + n * 128
                target = (3 * n + part) * 128
                sent_ref[device, :, target : target + 128] = qkv_ref[:, source : source + 128]
        if device % 2 == 0:
            sent_ref[device, :, 3 * own :] = out_ref[:, :half]
        else:
            rest = 3 * own + width - half
            sent_ref[device, :, 3 * own : rest] = out_ref[:, half:]
            sent_ref[device, :, rest : rest + 128] = loc_ref[...]
            sent_ref[device, :, rest + 128 :] = mix.astype(BF16)


def prepare(w_qkv, w_out, w_loc, w_mix, devices):
    rows, width = w_out.shape
    columns = 3 * width // devices + (width + 256) // 2
    return pl.pallas_call(
        prepare_kernel,
        out_shape=jax.ShapeDtypeStruct((devices, rows, columns), BF16),
        name="prepare",
    )(w_qkv, w_out, w_loc, w_mix.T)


def attention_kernel(meta, *refs, pieces, weight_parts, own_slot, with_decode):
    refs = list(refs)
    xs = [refs.pop(0) for _ in range(pieces)]
    weights = [refs.pop(0) for _ in range(weight_parts)]
    gain_ref, table_ref, variate_ref = refs.pop(0), refs.pop(0), refs.pop(0)
    dec_ref = refs.pop(0) if with_decode else None
    out = refs.pop(0)
    xbuf, wbuf, keys, values, key_extra, queries, held, obuf, dec_held, xsems, wsems, osems = refs
    chunks = keys.shape[0] // 2
    fsdp_index, req_index, length = meta[0], meta[1], meta[2 + own_slot]
    block = pl.program_id(0)
    rows = xbuf.shape[1]
    tile = math.gcd(rows, 256)
    splits = 4
    per_step = 4
    part = rows // splits

    def fetch_part(source, slot, i):
        here = pl.ds(i * part, part)
        return pltpu.make_async_copy(source.at[here], xbuf.at[slot, here], xsems.at[slot, i])

    def fetch(which, slot):
        offset = which ^ fsdp_index
        for j in range(pieces):
            source = xs[j].at[own_slot] if j == 0 else xs[j]

            @pl.when(offset == j)
            def _():
                for i in range(splits):
                    fetch_part(source, slot, i).start()

    slot = lax.rem(block, 2)

    @pl.when(block == 0)
    def _():
        fetch(block, slot)
        for copy in weight_copies(weights, wbuf, wsems, req_index):
            copy.start()

    @pl.when(block + 1 < pieces)
    def _():
        fetch(block + 1, 1 - slot)

    for i in range(splits):
        fetch_part(xs[0].at[own_slot], slot, i).wait()
    normed = normalise(xbuf[slot], gain_ref[...])
    first_row = pl.multiple_of(block * rows, rows)
    here = pl.ds(first_row, rows)
    lane = lax.broadcasted_iota(jnp.int32, (rows, 128), 1)
    low = lane < 64
    variate = jnp.broadcast_to(variate_ref[own_slot : own_slot + 1, here].astype(F32), (128, rows)).T.astype(jnp.int32)
    same = (lane & 3) == variate
    position = first_row + lax.broadcasted_iota(jnp.int32, (rows, 128), 0)
    extra = jnp.where(
        lane < 12,
        jnp.where(same, 1.0, 0.0),
        jnp.where((lane == 12) & (position >= length), big_negative, 0.0),
    )
    key_extra[here, :] = extra.astype(BF16)

    @pl.when(block == 0)
    def _():
        for copy in weight_copies(weights, wbuf, wsems, req_index):
            copy.wait()
        if with_decode:
            dec_held[...] = jnp.zeros(dec_held.shape, F32)
            dec_held[: dec_ref.shape[0], :] = dec_ref[...].astype(F32)
            dec_rows = normalise(dec_held[...], gain_ref[...])
            dec_qkv = jnp.dot(dec_rows, wbuf[...], preferred_element_type=F32).astype(BF16)
            padded = dec_held.shape[0]
            for i in range(pieces):
                for n in range(chunks):
                    for which in range(3):
                        first = rows + which * padded
                        source = (3 * n + which) * 128
                        obuf[i, first : first + padded, n * 128 : (n + 1) * 128] = dec_qkv[
                            :, source : source + 128
                        ]

    everything = jnp.dot(normed, wbuf[...], preferred_element_type=F32)
    for n in range(chunks):
        projected = everything[:, n * 384 : (n + 1) * 384].astype(BF16)
        q = projected[:, :128].astype(F32) * (log2e * 0.125)
        k = projected[:, 128:256].astype(F32)
        v = projected[:, 256:].astype(F32)
        q_high = q.astype(BF16).astype(F32)
        q_low = q - q_high
        q_high_turned = pltpu.roll(q_high, 64, 1)
        q_low_turned = pltpu.roll(q_low, 64, 1)
        k_turned = pltpu.roll(k, 64, 1)
        keys[2 * n, here, :] = jnp.where(low, k, k_turned).astype(BF16)
        keys[2 * n + 1, here, :] = jnp.where(low, k_turned, k).astype(BF16)
        values[2 * n, here, :] = jnp.where(low, v, 1.0).astype(BF16)
        values[2 * n + 1, here, :] = jnp.where(low, 1.0, v).astype(BF16)
        for half, q_main in (
            (0, jnp.where(low, q_high, q_low_turned)),
            (1, jnp.where(low, q_high_turned, q_low)),
        ):
            bias = table_ref[2 * n + half]
            q_extra = jnp.where(same, bias[0:1], bias[1:2])
            queries[2 * n + half, :, :128] = q_main.astype(BF16)
            queries[2 * n + half, :, 128:] = q_extra.astype(BF16)

    for c in range(pieces):

        @pl.when(block == c)
        def _(c=c):
            diagonal = lax.broadcasted_iota(jnp.int32, (tile, tile), 1) <= lax.broadcasted_iota(
                jnp.int32, (tile, tile), 0
            )
            def score(head, t):
                span = c * rows + (t + 1) * tile
                query = queries[head, t * tile : (t + 1) * tile, :]
                result = []
                for first, last in ((0, span - tile), (span - tile, span)):
                    if first < last:
                        key = jnp.concatenate(
                            [keys[head, first:last, :], key_extra[first:last, :]], axis=1
                        )
                        result.append(
                            lax.dot_general(query, key, NT, preferred_element_type=F32)
                        )
                result[-1] = jnp.where(diagonal, result[-1], big_negative)
                return result

            def mix(head, t, scores):
                top = functools.reduce(
                    jnp.maximum, [jnp.max(part, axis=1, keepdims=True) for part in scores]
                )
                total, first = 0.0, 0
                for part in scores:
                    last = first + part.shape[1]
                    total = total + jnp.dot(
                        jnp.exp2(part - top).astype(BF16),
                        values[head, first:last, :],
                        preferred_element_type=F32,
                    )
                    first = last
                mixed = total / pltpu.roll(total, 64, 1)
                held[head, t * tile : (t + 1) * tile, :] = mixed.astype(BF16)

            def some_heads(step, carry):
                units = [
                    (step * per_step + i, t) for i in range(per_step) for t in range(rows // tile)
                ]
                ready = score(*units[0])
                for i, unit in enumerate(units):
                    current = ready
                    if i + 1 < len(units):
                        ready = score(*units[i + 1])
                    mix(*unit, current)
                return carry

            lax.fori_loop(0, 2 * chunks // per_step, some_heads, 0)

    for n in range(chunks):
        obuf[block, :rows, n * 128 : (n + 1) * 128] = jnp.where(low, held[2 * n], held[2 * n + 1])
    pltpu.make_async_copy(obuf.at[block], out.at[block], osems.at[block]).start()

    @pl.when(block + 1 == pieces)
    def _():
        for i in range(pieces):
            pltpu.make_async_copy(obuf.at[i], out.at[i], osems.at[i]).wait()


def attention(meta, xs, own_slot, weights, gain, table, variates, dec_x=None):
    pieces, weight_parts = len(xs), len(weights)
    rows, width = xs[1].shape
    span = rows * pieces
    columns = weights[0].shape[-1]
    chunks = columns // 384
    with_decode = dec_x is not None
    whole = lambda shape: pl.BlockSpec(shape, lambda g, m: (0,) * len(shape))
    padded = dec_x.shape[0] + -dec_x.shape[0] % 16 if with_decode else 16
    out_rows = rows + (3 * padded if with_decode else 0)
    out_shape = jax.ShapeDtypeStruct((pieces, out_rows, chunks * 128), BF16)
    in_specs = [ANY] * (pieces + weight_parts) + [
        whole(gain.shape),
        whole(table.shape),
        whole(variates.shape),
    ]
    operands = list(xs) + list(weights) + [gain, table, variates]
    if with_decode:
        in_specs.append(whole(dec_x.shape))
        operands.append(dec_x)
    flops = 2 * span * width * columns + 2 * chunks * 4 * span * span * 128
    return pl.pallas_call(
        functools.partial(
            attention_kernel,
            pieces=pieces,
            weight_parts=weight_parts,
            own_slot=own_slot,
            with_decode=with_decode,
        ),
        out_shape=out_shape,
        grid_spec=pltpu.PrefetchScalarGridSpec(
            num_scalar_prefetch=1,
            grid=(pieces,),
            in_specs=in_specs,
            out_specs=ANY,
            scratch_shapes=[
                pltpu.VMEM((2, rows, width), BF16),
                pltpu.VMEM((width, columns), BF16),
                pltpu.VMEM((2 * chunks, span, 128), BF16),
                pltpu.VMEM((2 * chunks, span, 128), BF16),
                pltpu.VMEM((span, 128), BF16),
                pltpu.VMEM((2 * chunks, rows, 256), BF16),
                pltpu.VMEM((2 * chunks, rows, 128), BF16),
                pltpu.VMEM((pieces, out_rows, chunks * 128), BF16),
                pltpu.VMEM((padded, width), F32),
                pltpu.SemaphoreType.DMA((2, 4)),
                pltpu.SemaphoreType.DMA((weight_parts,)),
                pltpu.SemaphoreType.DMA((pieces,)),
            ],
        ),
        compiler_params=pltpu.CompilerParams(vmem_limit_bytes=60 * 2**20),
        cost_estimate=pl.CostEstimate(
            flops=flops, bytes_accessed=span * width * 2, transcendentals=chunks * span * span
        ),
        name="prefill",
    )(meta, *operands)


def decode_kernel(meta, groups, lengths, variates, *refs, sources, first_row):
    qkv_ref, refs = refs[0], refs[1:]
    same_ref, diff_ref, cache_ref, prompt_ref, cache_var_ref, prompt_var_ref, out_ref = refs[:7]
    got, held, sems = refs[7:]
    request = pl.program_id(0)
    fsdp_index = meta[0]
    length, variate = lengths[request], variates[request]
    width = out_ref.shape[-1]
    heads = same_ref.shape[1]
    size = width // heads
    own_width = width // sources
    padded = held.shape[1]

    @pl.when(request == 0)
    def _():
        copies = [
            pltpu.make_async_copy(
                qkv_ref.at[j, pl.ds(first_row, 3 * padded)], got.at[j], sems.at[j]
            )
            for j in range(sources)
        ]
        for copy in copies:
            copy.start()
        for copy in copies:
            copy.wait()
        for j in range(sources):
            for n in range(own_width // 128):
                for which in range(3):
                    column = j * own_width + n * 128
                    part = got[j, which * padded : (which + 1) * padded, n * 128 : (n + 1) * 128]
                    held[which, :, column : column + 128] = part.astype(F32)

    corner = lax.broadcasted_iota(jnp.int32, (heads, heads), 0) == lax.broadcasted_iota(
        jnp.int32, (heads, heads), 1
    )
    same_bias = jnp.sum(jnp.where(corner, same_ref[...], 0.0), axis=1, keepdims=True)
    diff_bias = jnp.sum(jnp.where(corner, diff_ref[...], 0.0), axis=1, keepdims=True)
    own_head = lax.broadcasted_iota(jnp.int32, (heads, width), 1) // size == lax.broadcasted_iota(
        jnp.int32, (heads, width), 0
    )
    row = pl.ds(request, 1)
    query, own_key, own_value = held[0, row, :], held[1, row, :], held[2, row, :]
    spread = jnp.where(own_head, query, 0.0)
    spread_low = spread.astype(BF16)
    scaling = 1.0 / math.sqrt(size)

    def scores(kv_ref, key_variates):
        raw = lax.dot_general(spread_low, kv_ref[0, :, :width], NT, preferred_element_type=F32)
        return raw * scaling + jnp.where(key_variates == variate, same_bias, diff_bias)

    cache_rows = cache_ref.shape[1]
    cache_scores = scores(cache_ref, cache_var_ref[pl.ds(request, 1), :])
    spot = fsdp_index * cache_rows + lax.broadcasted_iota(jnp.int32, (1, cache_rows), 1)
    valid = spot < length
    cache_scores = jnp.where(valid, cache_scores, big_negative)
    prompt_scores = scores(prompt_ref, prompt_var_ref[pl.ds(groups[request], 1), :])
    own_score = (
        jnp.sum(spread * own_key, axis=1, keepdims=True) * scaling + same_bias
    )
    own_score = jnp.where(fsdp_index == 0, own_score, big_negative)
    top = jnp.maximum(
        jnp.maximum(
            jnp.max(cache_scores, axis=1, keepdims=True), jnp.max(prompt_scores, axis=1, keepdims=True)
        ),
        own_score,
    )
    cache_weights = jnp.where(valid, jnp.exp(cache_scores - top), 0.0)
    prompt_weights = jnp.exp(prompt_scores - top)
    own_weight = jnp.where(fsdp_index == 0, jnp.exp(own_score - top), 0.0)
    total = (
        jnp.sum(cache_weights, axis=1, keepdims=True)
        + jnp.sum(prompt_weights, axis=1, keepdims=True)
        + own_weight
    )
    mixed = jnp.dot(cache_weights.astype(BF16), cache_ref[0, :, width:], preferred_element_type=F32)
    mixed = mixed + jnp.dot(
        prompt_weights.astype(BF16), prompt_ref[0, :, width:], preferred_element_type=F32
    )
    mixed = mixed + own_weight.astype(BF16).astype(F32) * own_value

    def pick(part):
        return jnp.sum(jnp.where(own_head, part, 0.0), axis=0, keepdims=True)

    out_ref[0, row, :] = pick(mixed)
    out_ref[1, row, :] = pick(top)
    out_ref[2, row, :] = pick(total)


def decode(
    meta, groups, lengths, variates, qkv, first_row, padded, biases, cache_kv, prompt_kv, key_variates
):
    requests, cache_rows, both = cache_kv.shape
    prompt_rows = prompt_kv.shape[1]
    width = both // 2
    sources = qkv.shape[0]
    whole = lambda array: pl.BlockSpec(array.shape, lambda r, *s: (0,) * array.ndim)
    return pl.pallas_call(
        functools.partial(decode_kernel, sources=sources, first_row=first_row),
        out_shape=jax.ShapeDtypeStruct((3, requests, width), F32),
        grid_spec=pltpu.PrefetchScalarGridSpec(
            num_scalar_prefetch=4,
            grid=(requests,),
            in_specs=[ANY]
            + [whole(bias) for bias in biases]
            + [
                pl.BlockSpec((1, cache_rows, both), lambda r, *s: (r, 0, 0)),
                pl.BlockSpec((1, prompt_rows, both), lambda r, m, g, *s: (g[r], 0, 0)),
            ]
            + [whole(ids) for ids in key_variates],
            out_specs=pl.BlockSpec((3, requests, width), lambda r, *s: (0, 0, 0)),
            scratch_shapes=[
                pltpu.VMEM((sources, 3 * padded, width // sources), BF16),
                pltpu.VMEM((3, padded, width), F32),
                pltpu.SemaphoreType.DMA((sources,)),
            ],
        ),
        compiler_params=pltpu.CompilerParams(vmem_limit_bytes=60 * 2**20),
        cost_estimate=pl.CostEstimate(
            flops=4 * requests * (cache_rows + prompt_rows) * width * 16,
            bytes_accessed=(cache_kv.size + requests * prompt_rows * both) * 2,
            transcendentals=0,
        ),
        name="decode",
    )(meta, groups, lengths, variates, qkv, *biases, cache_kv, prompt_kv, *key_variates)


def out_kernel(meta, *refs, sources, weight_parts, components, with_decode, aliased):
    refs = list(refs)
    x_ref = refs.pop(0)
    attn = refs.pop(0)
    weights = [[refs.pop(0) for _ in range(weight_parts)] for _ in range(2)]
    if with_decode:
        dec_x_ref = refs.pop(0)
        parts = [refs.pop(0) for _ in range(sources)]
    refs = refs[aliased:]
    out_ref, fore_ref = refs.pop(0), refs.pop(0)
    if with_decode:
        dec_out_ref, dec_fore_ref = refs.pop(0), refs.pop(0)
    abuf, wbuf, asems, wsems = refs
    fsdp_index, req_index = meta[0], meta[1]
    step = pl.program_id(0)
    tile, width = x_ref.shape[1:]
    own_width = width // sources
    half = wbuf.shape[2]

    def copies():
        result = []
        for i in range(2):
            target = wbuf.at[(fsdp_index & 1) ^ i]
            flat = [piece.at[j] for j in range(weights[i][0].shape[0]) for piece in weights[i]]
            result += weight_copies(flat, target, wsems.at[i], req_index)
        for j in range(sources):
            result.append(
                pltpu.make_async_copy(
                    attn.at[j, pl.ds(0, abuf.shape[0])],
                    abuf.at[:, pl.ds(j * own_width, own_width)],
                    asems.at[j],
                )
            )
        return result

    def finish(rows_in, mixed_in):
        left = jnp.dot(mixed_in, wbuf[0], preferred_element_type=F32)
        right = jnp.dot(mixed_in, wbuf[1, :, : width - half], preferred_element_type=F32)
        result = (rows_in.astype(F32) + jnp.concatenate([left, right], axis=1)).astype(BF16)
        scaled = normalise(result, None)
        both = jnp.dot(scaled, wbuf[1, :, width - half :], preferred_element_type=F32)
        centers, logits = both[:, :128], both[:, 128:]
        group = 128 // components

        def around(part, join):
            shift = group
            while shift < 128:
                part = join(part, pltpu.roll(part, shift, 1))
                shift *= 2
            return part

        weights_mix = jnp.exp(logits - around(logits, jnp.maximum))
        share = weights_mix / around(weights_mix, jnp.add)
        return result, around(share * centers, jnp.add)[:, :group]

    @pl.when(step == 0)
    def _():
        for copy in copies():
            copy.start()
        for copy in copies():
            copy.wait()
        if with_decode:
            top = functools.reduce(jnp.maximum, [part[1] for part in parts])
            total = jnp.zeros_like(top)
            mixed = jnp.zeros_like(top)
            for part in parts:
                factor = jnp.exp(part[1] - top)
                total = total + part[2] * factor
                mixed = mixed + part[0] * factor
            result, fore = finish(dec_x_ref[...], (mixed / total).astype(BF16))
            dec_out_ref[...] = result
            dec_fore_ref[...] = fore

    here = pl.ds(pl.multiple_of(step * tile, tile), tile)
    result, fore = finish(x_ref[0], abuf[here, :])
    out_ref[0] = result
    fore_ref[0] = fore


def finish_rows(meta, run, stretch_x, attn, weights, components, previous=(), dec_x=None, parts=()):
    runs, rows, width = stretch_x.shape
    sources = attn.shape[0]
    weight_parts = len(weights[0])
    group = 128 // components
    flat_weights = [part for parts_of in weights for part in parts_of]
    half = flat_weights[0].shape[-1]
    req_blocks = flat_weights[0].shape[0] * weight_parts
    tile = math.gcd(rows, 256)
    whole = lambda shape: pl.BlockSpec(shape, lambda g, m: (0,) * len(shape))
    with_decode = dec_x is not None
    out_shape = [
        jax.ShapeDtypeStruct((runs, rows, width), BF16),
        jax.ShapeDtypeStruct((runs, rows, group), F32),
    ]
    out_specs = [
        pl.BlockSpec((1, tile, width), lambda g, m: (run, g, 0)),
        pl.BlockSpec((1, tile, group), lambda g, m: (run, g, 0)),
    ]
    operands = [stretch_x, attn, *flat_weights]
    in_specs = [pl.BlockSpec((1, tile, width), lambda g, m: (run, g, 0))] + [ANY] * (len(operands) - 1)
    if with_decode:
        operands += [dec_x, *parts]
        in_specs += [whole(dec_x.shape)] + [whole(part.shape) for part in parts]
        out_shape += [
            jax.ShapeDtypeStruct(dec_x.shape, BF16),
            jax.ShapeDtypeStruct((dec_x.shape[0], group), F32),
        ]
        out_specs += [whole(shape.shape) for shape in out_shape[2:]]
    aliases = {1 + len(operands) + i: i for i in range(len(previous))}
    operands += list(previous)
    in_specs += [ANY] * len(previous)
    return pl.pallas_call(
        functools.partial(
            out_kernel,
            sources=sources,
            weight_parts=weight_parts,
            components=components,
            with_decode=with_decode,
            aliased=len(previous),
        ),
        out_shape=out_shape,
        grid_spec=pltpu.PrefetchScalarGridSpec(
            num_scalar_prefetch=1,
            grid=(rows // tile,),
            in_specs=in_specs,
            out_specs=out_specs,
            scratch_shapes=[
                pltpu.VMEM((rows, width), BF16),
                pltpu.VMEM((2, width, half), BF16),
                pltpu.SemaphoreType.DMA((sources,)),
                pltpu.SemaphoreType.DMA((2, req_blocks)),
            ],
        ),
        input_output_aliases=aliases,
        compiler_params=pltpu.CompilerParams(vmem_limit_bytes=60 * 2**20),
        cost_estimate=pl.CostEstimate(
            flops=2 * rows * width * (width + 256),
            bytes_accessed=3 * rows * width * 2,
            transcendentals=0,
        ),
        name="finish",
    )(meta, *operands)


def bias_table(bias_same, bias_diff):
    both = jnp.stack([bias_same, bias_diff], axis=1) * log2e
    terms = []
    rest = both
    for _ in range(3):
        term = lax.reduce_precision(rest, 8, 7)
        terms.append(term)
        rest = rest - term
    lanes = jnp.repeat(jnp.stack(terms, axis=-1), 4, axis=-1)
    ones = jnp.ones(both.shape + (1,), F32)
    zeros = jnp.zeros(both.shape + (115,), F32)
    return jnp.concatenate([lanes, ones, zeros], axis=-1)


def shards(
    stretch_x,
    dec_x,
    w_qkv,
    w_out,
    w_loc,
    w_mix,
    attn_gain,
    bias_same,
    bias_diff,
    cache_kv,
    prompt_kv,
    stretch_len,
    cache_len,
    prompt_group,
    pre_variate,
    dec_variate,
    cache_variate,
    prompt_variate,
    *,
    req_size,
    fsdp_size,
):
    runs, rows, width = stretch_x.shape
    heads = bias_same.shape[0]
    components = w_mix.shape[1]
    fsdp_index = lax.axis_index("fsdp").astype(jnp.int32)
    req_index = lax.axis_index("req").astype(jnp.int32)
    own_heads = heads // fsdp_size
    own_width = width // fsdp_size
    after = lambda value, *others: lax.optimization_barrier((value,) + others)[0]
    permute = lambda value, offset: swap(value, "fsdp", fsdp_size, offset)

    w_rows = w_qkv.shape[0]
    sent = prepare(w_qkv, w_out, w_loc, w_mix, fsdp_size)
    sent = lax.all_to_all(sent, "fsdp", 0, 0, tiled=True).reshape(fsdp_size * w_rows, -1)
    gain = attn_gain.reshape(1, width)
    table = bias_table(bias_same, bias_diff)
    table = lax.dynamic_slice_in_dim(table, fsdp_index * own_heads, own_heads, 0)

    meta = jnp.concatenate([jnp.stack([fsdp_index, req_index]), stretch_len])
    sent, meta, table = lax.optimization_barrier((sent, meta, table))
    w_pieces = {0: sent[:, : 3 * own_width]}
    for j in range(2, req_size, 2):
        w_pieces[j] = swap(w_pieces[0], "req", req_size, j)
    for j in range(0, req_size, 2):
        w_pieces[j + 1] = swap(w_pieces[j], "req", req_size, 1)
    w_pieces = [w_pieces[j] for j in range(req_size)]

    def gather_start(own, *others):
        own = after(own, *others)
        return {0: own, fsdp_size // 2: permute(own, fsdp_size // 2)}

    def gather_rest(got):
        offset = fsdp_size // 4
        while offset:
            for j, part in list(got.items()):
                got[j | offset] = permute(part, offset)
            offset //= 2
        return [got[j] for j in range(fsdp_size)]

    x_started = [gather_start(stretch_x[0], sent)]
    for run in range(1, runs):
        x_started.append(gather_start(stretch_x[run], x_started[-1][fsdp_size // 2], *w_pieces))

    returned = []
    for run in range(runs):
        got = x_started[run]
        wait = [attn] if run else w_pieces
        got = {j: after(part, *wait) if j else part for j, part in got.items()}
        x_pieces = gather_rest(got)
        attn = attention(
            meta,
            [stretch_x] + x_pieces[1:],
            run,
            w_pieces,
            gain,
            table,
            pre_variate,
            dec_x if run == 0 else None,
        )
        returned.append(lax.all_to_all(attn, "fsdp", 0, 0, tiled=True))
        if run == 0:
            others = after(sent[:, 3 * own_width :], attn)
            pair = jnp.stack([others, swap(others, "req", req_size, 1)])

    pairs = [pair] + [swap(pair, "req", req_size, j) for j in range(2, req_size, 2)]
    w_own = jnp.concatenate([after(pairs[0], attn)] + pairs[1:], axis=0)
    weights = [[w_own], [permute(w_own, 1)]]

    partial = decode(
        meta,
        after(prompt_group, attn),
        cache_len,
        dec_variate,
        returned[0],
        rows,
        dec_x.shape[0] + -dec_x.shape[0] % 16,
        [bias_same.reshape(1, heads), bias_diff.reshape(1, heads)],
        cache_kv,
        prompt_kv,
        [cache_variate, prompt_variate],
    )
    parts = [partial] + [permute(partial, j) for j in range(1, fsdp_size)]

    returned[0] = after(returned[0], partial)
    done = ()
    for run in range(runs - 1):
        done = finish_rows(meta, run, stretch_x, returned[run], weights, components, done)
    pre_out, pre_fore, dec_out, dec_fore = finish_rows(
        meta, runs - 1, stretch_x, returned[-1], weights, components, done, dec_x, parts
    )
    return pre_out, dec_out, pre_fore, dec_fore


def solution(mesh):
    return jax.shard_map(
        functools.partial(shards, req_size=mesh.shape["req"], fsdp_size=mesh.shape["fsdp"]),
        mesh=mesh,
        in_specs=(
            P("req", "fsdp", None),
            P("req", None),
            P(("req", "fsdp"), None),
            P(("req", "fsdp"), None),
            P(("req", "fsdp"), None),
            P(("req", "fsdp"), None),
            P(),
            P(),
            P(),
            P("req", "fsdp", None),
            P(None, "fsdp", None),
            P("req"),
            P("req"),
            P("req"),
            P("req", None),
            P("req"),
            P("req", "fsdp"),
            P(None, "fsdp"),
        ),
        out_specs=(P("req", "fsdp", None), P("req", None), P("req", "fsdp", None), P("req", None)),
        check_vma=False,
    )
```

```python
import functools
import math

import jax
import jax.numpy as jnp
from jax import lax
from jax.experimental import pallas as pl
from jax.experimental.pallas import tpu as pltpu
from jax.sharding import PartitionSpec as P

epsilon = 1e-05
big_negative = -1e30
log2e = math.log2(math.e)
F32 = jnp.float32
BF16 = jnp.bfloat16
ANY = pl.BlockSpec(memory_space=pl.ANY)
VMEM = pl.BlockSpec(memory_space=pltpu.VMEM)
NT = (((1,), (1,)), ((), ()))


def swap(value, axis, size, offset):
    return lax.ppermute(value, axis, [(i, i ^ offset) for i in range(size)])


def normalise(rows, gain):
    as_float = rows.astype(F32)
    factor = lax.rsqrt(jnp.mean(as_float * as_float, axis=-1, keepdims=True) + epsilon)
    scaled = as_float * factor
    return (scaled if gain is None else scaled * gain).astype(BF16)


def weight_copies(pieces, target, sems, req_index):
    copies = []
    for j, piece in enumerate(pieces):
        rows = piece.shape[0]
        first = pl.multiple_of((req_index ^ j) * rows, rows)
        copies.append(pltpu.make_async_copy(piece, target.at[pl.ds(first, rows)], sems.at[j]))
    return copies


def prepare_kernel(qkv_ref, out_ref, loc_ref, mix_ref, sent_ref):
    devices = sent_ref.shape[0]
    width = out_ref.shape[1]
    own = width // devices
    half = sent_ref.shape[2] - 3 * own
    components = mix_ref.shape[0]
    pick = lax.broadcasted_iota(jnp.int32, (components, 128), 1) // (
        128 // components
    ) == lax.broadcasted_iota(jnp.int32, (components, 128), 0)
    mix = lax.dot_general(
        mix_ref[...], pick.astype(BF16), (((0,), (0,)), ((), ())), preferred_element_type=F32
    )
    for device in range(devices):
        for n in range(own // 128):
            for part in range(3):
                source = part * width + device * own + n * 128
                target = (3 * n + part) * 128
                sent_ref[device, :, target : target + 128] = qkv_ref[:, source : source + 128]
        if device % 2 == 0:
            sent_ref[device, :, 3 * own :] = out_ref[:, :half]
        else:
            rest = 3 * own + width - half
            sent_ref[device, :, 3 * own : rest] = out_ref[:, half:]
            sent_ref[device, :, rest : rest + 128] = loc_ref[...]
            sent_ref[device, :, rest + 128 :] = mix.astype(BF16)


def prepare(w_qkv, w_out, w_loc, w_mix, devices):
    rows, width = w_out.shape
    columns = 3 * width // devices + (width + 256) // 2
    return pl.pallas_call(
        prepare_kernel,
        out_shape=jax.ShapeDtypeStruct((devices, rows, columns), BF16),
        name="prepare",
    )(w_qkv, w_out, w_loc, w_mix.T)


def attention_kernel(meta, *refs, pieces, weight_parts, own_slot, with_decode):
    refs = list(refs)
    xs = [refs.pop(0) for _ in range(pieces)]
    weights = [refs.pop(0) for _ in range(weight_parts)]
    gain_ref, table_ref, variate_ref = refs.pop(0), refs.pop(0), refs.pop(0)
    dec_ref = refs.pop(0) if with_decode else None
    out = refs.pop(0)
    xbuf, wbuf, keys, values, key_extra, queries, held, obuf, dec_held, xsems, wsems, osems = refs
    chunks = keys.shape[0] // 2
    fsdp_index, req_index, length = meta[0], meta[1], meta[2 + own_slot]
    block = pl.program_id(0)
    rows = xbuf.shape[1]
    tile = math.gcd(rows, 256)
    splits = 4
    per_step = 4
    part = rows // splits

    def fetch_part(source, slot, i):
        here = pl.ds(i * part, part)
        return pltpu.make_async_copy(source.at[here], xbuf.at[slot, here], xsems.at[slot, i])

    def fetch(which, slot):
        offset = which ^ fsdp_index
        for j in range(pieces):
            source = xs[j].at[own_slot] if j == 0 else xs[j]

            @pl.when(offset == j)
            def _():
                for i in range(splits):
                    fetch_part(source, slot, i).start()

    slot = lax.rem(block, 2)

    @pl.when(block == 0)
    def _():
        fetch(block, slot)
        for copy in weight_copies(weights, wbuf, wsems, req_index):
            copy.start()

    @pl.when(block + 1 < pieces)
    def _():
        fetch(block + 1, 1 - slot)

    for i in range(splits):
        fetch_part(xs[0].at[own_slot], slot, i).wait()
    normed = normalise(xbuf[slot], gain_ref[...])
    first_row = pl.multiple_of(block * rows, rows)
    here = pl.ds(first_row, rows)
    lane = lax.broadcasted_iota(jnp.int32, (rows, 128), 1)
    low = lane < 64
    variate = jnp.broadcast_to(variate_ref[own_slot : own_slot + 1, here].astype(F32), (128, rows)).T.astype(jnp.int32)
    same = (lane & 3) == variate
    position = first_row + lax.broadcasted_iota(jnp.int32, (rows, 128), 0)
    extra = jnp.where(
        lane < 12,
        jnp.where(same, 1.0, 0.0),
        jnp.where((lane == 12) & (position >= length), big_negative, 0.0),
    )
    key_extra[here, :] = extra.astype(BF16)

    @pl.when(block == 0)
    def _():
        for copy in weight_copies(weights, wbuf, wsems, req_index):
            copy.wait()
        if with_decode:
            dec_held[...] = jnp.zeros(dec_held.shape, F32)
            dec_held[: dec_ref.shape[0], :] = dec_ref[...].astype(F32)
            dec_rows = normalise(dec_held[...], gain_ref[...])
            dec_qkv = jnp.dot(dec_rows, wbuf[...], preferred_element_type=F32).astype(BF16)
            padded = dec_held.shape[0]
            for i in range(pieces):
                for n in range(chunks):
                    for which in range(3):
                        first = rows + which * padded
                        source = (3 * n + which) * 128
                        obuf[i, first : first + padded, n * 128 : (n + 1) * 128] = dec_qkv[
                            :, source : source + 128
                        ]

    everything = jnp.dot(normed, wbuf[...], preferred_element_type=F32)
    for n in range(chunks):
        projected = everything[:, n * 384 : (n + 1) * 384].astype(BF16)
        q = projected[:, :128].astype(F32) * (log2e * 0.125)
        k = projected[:, 128:256].astype(F32)
        v = projected[:, 256:].astype(F32)
        q_high = q.astype(BF16).astype(F32)
        q_low = q - q_high
        q_high_turned = pltpu.roll(q_high, 64, 1)
        q_low_turned = pltpu.roll(q_low, 64, 1)
        k_turned = pltpu.roll(k, 64, 1)
        keys[2 * n, here, :] = jnp.where(low, k, k_turned).astype(BF16)
        keys[2 * n + 1, here, :] = jnp.where(low, k_turned, k).astype(BF16)
        values[2 * n, here, :] = jnp.where(low, v, 1.0).astype(BF16)
        values[2 * n + 1, here, :] = jnp.where(low, 1.0, v).astype(BF16)
        for half, q_main in (
            (0, jnp.where(low, q_high, q_low_turned)),
            (1, jnp.where(low, q_high_turned, q_low)),
        ):
            bias = table_ref[2 * n + half]
            q_extra = jnp.where(same, bias[0:1], bias[1:2])
            queries[2 * n + half, :, :128] = q_main.astype(BF16)
            queries[2 * n + half, :, 128:] = q_extra.astype(BF16)

    for c in range(pieces):

        @pl.when(block == c)
        def _(c=c):
            diagonal = lax.broadcasted_iota(jnp.int32, (tile, tile), 1) <= lax.broadcasted_iota(
                jnp.int32, (tile, tile), 0
            )
            def score(head, t):
                span = c * rows + (t + 1) * tile
                query = queries[head, t * tile : (t + 1) * tile, :]
                result = []
                for first, last in ((0, span - tile), (span - tile, span)):
                    if first < last:
                        key = jnp.concatenate(
                            [keys[head, first:last, :], key_extra[first:last, :]], axis=1
                        )
                        result.append(
                            lax.dot_general(query, key, NT, preferred_element_type=F32)
                        )
                result[-1] = jnp.where(diagonal, result[-1], big_negative)
                return result

            def mix(head, t, scores):
                top = functools.reduce(
                    jnp.maximum, [jnp.max(part, axis=1, keepdims=True) for part in scores]
                )
                total, first = 0.0, 0
                for part in scores:
                    last = first + part.shape[1]
                    total = total + jnp.dot(
                        jnp.exp2(part - top).astype(BF16),
                        values[head, first:last, :],
                        preferred_element_type=F32,
                    )
                    first = last
                mixed = total / pltpu.roll(total, 64, 1)
                held[head, t * tile : (t + 1) * tile, :] = mixed.astype(BF16)

            def some_heads(step, carry):
                units = [
                    (step * per_step + i, t) for i in range(per_step) for t in range(rows // tile)
                ]
                ready = score(*units[0])
                for i, unit in enumerate(units):
                    current = ready
                    if i + 1 < len(units):
                        ready = score(*units[i + 1])
                    mix(*unit, current)
                return carry

            lax.fori_loop(0, 2 * chunks // per_step, some_heads, 0)

    for n in range(chunks):
        obuf[block, :rows, n * 128 : (n + 1) * 128] = jnp.where(low, held[2 * n], held[2 * n + 1])
    pltpu.make_async_copy(obuf.at[block], out.at[block], osems.at[block]).start()

    @pl.when(block + 1 == pieces)
    def _():
        for i in range(pieces):
            pltpu.make_async_copy(obuf.at[i], out.at[i], osems.at[i]).wait()


def attention(meta, xs, own_slot, weights, gain, table, variates, dec_x=None):
    pieces, weight_parts = len(xs), len(weights)
    rows, width = xs[1].shape
    span = rows * pieces
    columns = weights[0].shape[-1]
    chunks = columns // 384
    with_decode = dec_x is not None
    whole = lambda shape: pl.BlockSpec(shape, lambda g, m: (0,) * len(shape))
    padded = dec_x.shape[0] + -dec_x.shape[0] % 16 if with_decode else 16
    out_rows = rows + (3 * padded if with_decode else 0)
    out_shape = jax.ShapeDtypeStruct((pieces, out_rows, chunks * 128), BF16)
    in_specs = [ANY] * (pieces + weight_parts) + [
        whole(gain.shape),
        whole(table.shape),
        whole(variates.shape),
    ]
    operands = list(xs) + list(weights) + [gain, table, variates]
    if with_decode:
        in_specs.append(whole(dec_x.shape))
        operands.append(dec_x)
    flops = 2 * span * width * columns + 2 * chunks * 4 * span * span * 128
    return pl.pallas_call(
        functools.partial(
            attention_kernel,
            pieces=pieces,
            weight_parts=weight_parts,
            own_slot=own_slot,
            with_decode=with_decode,
        ),
        out_shape=out_shape,
        grid_spec=pltpu.PrefetchScalarGridSpec(
            num_scalar_prefetch=1,
            grid=(pieces,),
            in_specs=in_specs,
            out_specs=ANY,
            scratch_shapes=[
                pltpu.VMEM((2, rows, width), BF16),
                pltpu.VMEM((width, columns), BF16),
                pltpu.VMEM((2 * chunks, span, 128), BF16),
                pltpu.VMEM((2 * chunks, span, 128), BF16),
                pltpu.VMEM((span, 128), BF16),
                pltpu.VMEM((2 * chunks, rows, 256), BF16),
                pltpu.VMEM((2 * chunks, rows, 128), BF16),
                pltpu.VMEM((pieces, out_rows, chunks * 128), BF16),
                pltpu.VMEM((padded, width), F32),
                pltpu.SemaphoreType.DMA((2, 4)),
                pltpu.SemaphoreType.DMA((weight_parts,)),
                pltpu.SemaphoreType.DMA((pieces,)),
            ],
        ),
        compiler_params=pltpu.CompilerParams(vmem_limit_bytes=60 * 2**20),
        cost_estimate=pl.CostEstimate(
            flops=flops, bytes_accessed=span * width * 2, transcendentals=chunks * span * span
        ),
        name="prefill",
    )(meta, *operands)


def decode_kernel(meta, groups, lengths, variates, *refs, sources, first_row):
    qkv_ref, refs = refs[0], refs[1:]
    same_ref, diff_ref, cache_ref, prompt_ref, cache_var_ref, prompt_var_ref, out_ref = refs[:7]
    got, held, sems = refs[7:]
    request = pl.program_id(0)
    fsdp_index = meta[0]
    length, variate = lengths[request], variates[request]
    width = out_ref.shape[-1]
    heads = same_ref.shape[1]
    size = width // heads
    own_width = width // sources
    padded = held.shape[1]

    @pl.when(request == 0)
    def _():
        copies = [
            pltpu.make_async_copy(
                qkv_ref.at[j, pl.ds(first_row, 3 * padded)], got.at[j], sems.at[j]
            )
            for j in range(sources)
        ]
        for copy in copies:
            copy.start()
        for copy in copies:
            copy.wait()
        for j in range(sources):
            for n in range(own_width // 128):
                for which in range(3):
                    column = j * own_width + n * 128
                    part = got[j, which * padded : (which + 1) * padded, n * 128 : (n + 1) * 128]
                    held[which, :, column : column + 128] = part.astype(F32)

    corner = lax.broadcasted_iota(jnp.int32, (heads, heads), 0) == lax.broadcasted_iota(
        jnp.int32, (heads, heads), 1
    )
    same_bias = jnp.sum(jnp.where(corner, same_ref[...], 0.0), axis=1, keepdims=True)
    diff_bias = jnp.sum(jnp.where(corner, diff_ref[...], 0.0), axis=1, keepdims=True)
    own_head = lax.broadcasted_iota(jnp.int32, (heads, width), 1) // size == lax.broadcasted_iota(
        jnp.int32, (heads, width), 0
    )
    row = pl.ds(request, 1)
    query, own_key, own_value = held[0, row, :], held[1, row, :], held[2, row, :]
    spread = jnp.where(own_head, query, 0.0)
    spread_low = spread.astype(BF16)
    scaling = 1.0 / math.sqrt(size)

    def scores(kv_ref, key_variates):
        raw = lax.dot_general(spread_low, kv_ref[0, :, :width], NT, preferred_element_type=F32)
        return raw * scaling + jnp.where(key_variates == variate, same_bias, diff_bias)

    cache_rows = cache_ref.shape[1]
    cache_scores = scores(cache_ref, cache_var_ref[pl.ds(request, 1), :])
    spot = fsdp_index * cache_rows + lax.broadcasted_iota(jnp.int32, (1, cache_rows), 1)
    valid = spot < length
    cache_scores = jnp.where(valid, cache_scores, big_negative)
    prompt_scores = scores(prompt_ref, prompt_var_ref[pl.ds(groups[request], 1), :])
    own_score = (
        jnp.sum(spread * own_key, axis=1, keepdims=True) * scaling + same_bias
    )
    own_score = jnp.where(fsdp_index == 0, own_score, big_negative)
    top = jnp.maximum(
        jnp.maximum(
            jnp.max(cache_scores, axis=1, keepdims=True), jnp.max(prompt_scores, axis=1, keepdims=True)
        ),
        own_score,
    )
    cache_weights = jnp.where(valid, jnp.exp(cache_scores - top), 0.0)
    prompt_weights = jnp.exp(prompt_scores - top)
    own_weight = jnp.where(fsdp_index == 0, jnp.exp(own_score - top), 0.0)
    total = (
        jnp.sum(cache_weights, axis=1, keepdims=True)
        + jnp.sum(prompt_weights, axis=1, keepdims=True)
        + own_weight
    )
    mixed = jnp.dot(cache_weights.astype(BF16), cache_ref[0, :, width:], preferred_element_type=F32)
    mixed = mixed + jnp.dot(
        prompt_weights.astype(BF16), prompt_ref[0, :, width:], preferred_element_type=F32
    )
    mixed = mixed + own_weight.astype(BF16).astype(F32) * own_value

    def pick(part):
        return jnp.sum(jnp.where(own_head, part, 0.0), axis=0, keepdims=True)

    out_ref[0, row, :] = pick(mixed)
    out_ref[1, row, :] = pick(top)
    out_ref[2, row, :] = pick(total)


def decode(
    meta, groups, lengths, variates, qkv, first_row, padded, biases, cache_kv, prompt_kv, key_variates
):
    requests, cache_rows, both = cache_kv.shape
    prompt_rows = prompt_kv.shape[1]
    width = both // 2
    sources = qkv.shape[0]
    whole = lambda array: pl.BlockSpec(array.shape, lambda r, *s: (0,) * array.ndim)
    return pl.pallas_call(
        functools.partial(decode_kernel, sources=sources, first_row=first_row),
        out_shape=jax.ShapeDtypeStruct((3, requests, width), F32),
        grid_spec=pltpu.PrefetchScalarGridSpec(
            num_scalar_prefetch=4,
            grid=(requests,),
            in_specs=[ANY]
            + [whole(bias) for bias in biases]
            + [
                pl.BlockSpec((1, cache_rows, both), lambda r, *s: (r, 0, 0)),
                pl.BlockSpec((1, prompt_rows, both), lambda r, m, g, *s: (g[r], 0, 0)),
            ]
            + [whole(ids) for ids in key_variates],
            out_specs=pl.BlockSpec((3, requests, width), lambda r, *s: (0, 0, 0)),
            scratch_shapes=[
                pltpu.VMEM((sources, 3 * padded, width // sources), BF16),
                pltpu.VMEM((3, padded, width), F32),
                pltpu.SemaphoreType.DMA((sources,)),
            ],
        ),
        compiler_params=pltpu.CompilerParams(vmem_limit_bytes=60 * 2**20),
        cost_estimate=pl.CostEstimate(
            flops=4 * requests * (cache_rows + prompt_rows) * width * 16,
            bytes_accessed=(cache_kv.size + requests * prompt_rows * both) * 2,
            transcendentals=0,
        ),
        name="decode",
    )(meta, groups, lengths, variates, qkv, *biases, cache_kv, prompt_kv, *key_variates)


def out_kernel(meta, *refs, runs, sources, weight_parts, components):
    refs = list(refs)
    x_ref = refs.pop(0)
    attn = [refs.pop(0) for _ in range(runs)]
    weights = [[refs.pop(0) for _ in range(weight_parts)] for _ in range(2)]
    dec_x_ref = refs.pop(0)
    parts = [refs.pop(0) for _ in range(sources)]
    out_ref, fore_ref, dec_out_ref, dec_fore_ref, abuf, wbuf, asems, wsems = refs
    fsdp_index, req_index = meta[0], meta[1]
    step = pl.program_id(0)
    tile, width = x_ref.shape[1:]
    own_width = width // sources
    half = wbuf.shape[2]
    rows = abuf.shape[1]
    tiles = rows // tile

    def w_copies():
        result = []
        for i in range(2):
            target = wbuf.at[(fsdp_index & 1) ^ i]
            flat = [piece.at[j] for j in range(weights[i][0].shape[0]) for piece in weights[i]]
            result += weight_copies(flat, target, wsems.at[i], req_index)
        return result

    def a_copies(run):
        return [
            pltpu.make_async_copy(
                attn[run].at[j, pl.ds(0, rows)],
                abuf.at[run, :, pl.ds(j * own_width, own_width)],
                asems.at[run, j],
            )
            for j in range(sources)
        ]

    def finish(rows_in, mixed_in):
        left = jnp.dot(mixed_in, wbuf[0], preferred_element_type=F32)
        right = jnp.dot(mixed_in, wbuf[1, :, : width - half], preferred_element_type=F32)
        result = (rows_in.astype(F32) + jnp.concatenate([left, right], axis=1)).astype(BF16)
        scaled = normalise(result, None)
        both = jnp.dot(scaled, wbuf[1, :, width - half :], preferred_element_type=F32)
        centers, logits = both[:, :128], both[:, 128:]
        group = 128 // components

        def around(part, join):
            shift = group
            while shift < 128:
                part = join(part, pltpu.roll(part, shift, 1))
                shift *= 2
            return part

        weights_mix = jnp.exp(logits - around(logits, jnp.maximum))
        share = weights_mix / around(weights_mix, jnp.add)
        return result, around(share * centers, jnp.add)[:, :group]

    @pl.when(step == 0)
    def _():
        copies = a_copies(0) + w_copies()
        for run in range(1, runs):
            copies += a_copies(run)
        for copy in copies:
            copy.start()
        for copy in w_copies():
            copy.wait()

    for run in range(runs):

        @pl.when(step == run * tiles)
        def _(run=run):
            for copy in a_copies(run):
                copy.wait()

    here = pl.ds(pl.multiple_of(lax.rem(step, tiles) * tile, tile), tile)
    result, fore = finish(x_ref[0], abuf[step // tiles, here, :])
    out_ref[0] = result
    fore_ref[0] = fore

    @pl.when(step == runs * tiles - 1)
    def _():
        top = functools.reduce(jnp.maximum, [part[1] for part in parts])
        total = jnp.zeros_like(top)
        mixed = jnp.zeros_like(top)
        for part in parts:
            factor = jnp.exp(part[1] - top)
            total = total + part[2] * factor
            mixed = mixed + part[0] * factor
        result, fore = finish(dec_x_ref[...], (mixed / total).astype(BF16))
        dec_out_ref[...] = result
        dec_fore_ref[...] = fore


def finish_rows(meta, stretch_x, attn, weights, components, dec_x, parts):
    runs, rows, width = stretch_x.shape
    sources = attn[0].shape[0]
    weight_parts = len(weights[0])
    group = 128 // components
    flat_weights = [part for parts_of in weights for part in parts_of]
    half = flat_weights[0].shape[-1]
    req_blocks = flat_weights[0].shape[0] * weight_parts
    tile = rows
    tiles = rows // tile
    whole = lambda shape: pl.BlockSpec(shape, lambda g, m: (0,) * len(shape))
    by_rows = lambda last: pl.BlockSpec((1, tile, last), lambda g, m: (g // tiles, g % tiles, 0))
    operands = [stretch_x, *attn, *flat_weights, dec_x, *parts]
    return pl.pallas_call(
        functools.partial(
            out_kernel,
            runs=runs,
            sources=sources,
            weight_parts=weight_parts,
            components=components,
        ),
        out_shape=[
            jax.ShapeDtypeStruct((runs, rows, width), BF16),
            jax.ShapeDtypeStruct((runs, rows, group), F32),
            jax.ShapeDtypeStruct(dec_x.shape, BF16),
            jax.ShapeDtypeStruct((dec_x.shape[0], group), F32),
        ],
        grid_spec=pltpu.PrefetchScalarGridSpec(
            num_scalar_prefetch=1,
            grid=(runs * tiles,),
            in_specs=[by_rows(width)]
            + [ANY] * (runs + len(flat_weights))
            + [whole(dec_x.shape)]
            + [whole(part.shape) for part in parts],
            out_specs=[
                by_rows(width),
                by_rows(group),
                whole(dec_x.shape),
                whole((dec_x.shape[0], group)),
            ],
            scratch_shapes=[
                pltpu.VMEM((runs, rows, width), BF16),
                pltpu.VMEM((2, width, half), BF16),
                pltpu.SemaphoreType.DMA((runs, sources)),
                pltpu.SemaphoreType.DMA((2, req_blocks)),
            ],
        ),
        compiler_params=pltpu.CompilerParams(vmem_limit_bytes=60 * 2**20),
        cost_estimate=pl.CostEstimate(
            flops=2 * runs * rows * width * (width + 256),
            bytes_accessed=3 * runs * rows * width * 2,
            transcendentals=0,
        ),
        name="finish",
    )(meta, *operands)


def bias_table(bias_same, bias_diff):
    both = jnp.stack([bias_same, bias_diff], axis=1) * log2e
    terms = []
    rest = both
    for _ in range(3):
        term = lax.reduce_precision(rest, 8, 7)
        terms.append(term)
        rest = rest - term
    lanes = jnp.repeat(jnp.stack(terms, axis=-1), 4, axis=-1)
    ones = jnp.ones(both.shape + (1,), F32)
    zeros = jnp.zeros(both.shape + (115,), F32)
    return jnp.concatenate([lanes, ones, zeros], axis=-1)


def shards(
    stretch_x,
    dec_x,
    w_qkv,
    w_out,
    w_loc,
    w_mix,
    attn_gain,
    bias_same,
    bias_diff,
    cache_kv,
    prompt_kv,
    stretch_len,
    cache_len,
    prompt_group,
    pre_variate,
    dec_variate,
    cache_variate,
    prompt_variate,
    *,
    req_size,
    fsdp_size,
):
    runs, rows, width = stretch_x.shape
    heads = bias_same.shape[0]
    components = w_mix.shape[1]
    fsdp_index = lax.axis_index("fsdp").astype(jnp.int32)
    req_index = lax.axis_index("req").astype(jnp.int32)
    own_heads = heads // fsdp_size
    own_width = width // fsdp_size
    after = lambda value, *others: lax.optimization_barrier((value,) + others)[0]
    permute = lambda value, offset: swap(value, "fsdp", fsdp_size, offset)

    w_rows = w_qkv.shape[0]
    sent = prepare(w_qkv, w_out, w_loc, w_mix, fsdp_size)
    sent = lax.all_to_all(sent, "fsdp", 0, 0, tiled=True).reshape(fsdp_size * w_rows, -1)
    gain = attn_gain.reshape(1, width)
    table = bias_table(bias_same, bias_diff)
    table = lax.dynamic_slice_in_dim(table, fsdp_index * own_heads, own_heads, 0)

    meta = jnp.concatenate([jnp.stack([fsdp_index, req_index]), stretch_len])
    sent, meta, table = lax.optimization_barrier((sent, meta, table))
    w_pieces = {0: sent[:, : 3 * own_width]}
    for j in range(2, req_size, 2):
        w_pieces[j] = swap(w_pieces[0], "req", req_size, j)
    for j in range(0, req_size, 2):
        w_pieces[j + 1] = swap(w_pieces[j], "req", req_size, 1)
    w_pieces = [w_pieces[j] for j in range(req_size)]

    def gather_start(own, *others):
        own = after(own, *others)
        return {0: own, fsdp_size // 2: permute(own, fsdp_size // 2)}

    def gather_rest(got):
        offset = fsdp_size // 4
        while offset:
            for j, part in list(got.items()):
                got[j | offset] = permute(part, offset)
            offset //= 2
        return [got[j] for j in range(fsdp_size)]

    x_started = [gather_start(stretch_x[0], sent)]
    for run in range(1, runs):
        x_started.append(gather_start(stretch_x[run], x_started[-1][fsdp_size // 2], *w_pieces))

    returned = []
    for run in range(runs):
        got = x_started[run]
        wait = [attn] if run else w_pieces
        got = {j: after(part, *wait) if j else part for j, part in got.items()}
        x_pieces = gather_rest(got)
        attn = attention(
            meta,
            [stretch_x] + x_pieces[1:],
            run,
            w_pieces,
            gain,
            table,
            pre_variate,
            dec_x if run == 0 else None,
        )
        returned.append(lax.all_to_all(attn, "fsdp", 0, 0, tiled=True))
        if run == 0:
            others = after(sent[:, 3 * own_width :], attn)
            pair = jnp.stack([others, swap(others, "req", req_size, 1)])

    pairs = [pair] + [swap(pair, "req", req_size, j) for j in range(2, req_size, 2)]
    w_own = jnp.concatenate([after(pairs[0], attn)] + pairs[1:], axis=0)
    weights = [[w_own], [permute(w_own, 1)]]

    partial = decode(
        meta,
        after(prompt_group, attn),
        cache_len,
        dec_variate,
        returned[0],
        rows,
        dec_x.shape[0] + -dec_x.shape[0] % 16,
        [bias_same.reshape(1, heads), bias_diff.reshape(1, heads)],
        cache_kv,
        prompt_kv,
        [cache_variate, prompt_variate],
    )
    parts = [partial] + [permute(partial, j) for j in range(1, fsdp_size)]

    pre_out, pre_fore, dec_out, dec_fore = finish_rows(
        meta, stretch_x, returned, weights, components, dec_x, parts
    )
    return pre_out, dec_out, pre_fore, dec_fore


def solution(mesh):
    return jax.shard_map(
        functools.partial(shards, req_size=mesh.shape["req"], fsdp_size=mesh.shape["fsdp"]),
        mesh=mesh,
        in_specs=(
            P("req", "fsdp", None),
            P("req", None),
            P(("req", "fsdp"), None),
            P(("req", "fsdp"), None),
            P(("req", "fsdp"), None),
            P(("req", "fsdp"), None),
            P(),
            P(),
            P(),
            P("req", "fsdp", None),
            P(None, "fsdp", None),
            P("req"),
            P("req"),
            P("req"),
            P("req", None),
            P("req"),
            P("req", "fsdp"),
            P(None, "fsdp"),
        ),
        out_specs=(P("req", "fsdp", None), P("req", None), P("req", "fsdp", None), P("req", None)),
        check_vma=False,
    )
```
